32 devices in a mesh: genome: 8 (over z, x), samp: 4 (over y, core).
Axes of the slice: x: 2, y: 2, z: 4, core: 2. Of those that a mesh axis runs over, the one named last changes fastest.
Arguments:
- dosage: bfloat16 [16384, 8192], P('samp', 'genome'), may hold values from -6 to 6
- effects: bfloat16 [8192, 512], P('genome', 'samp'), may hold values from -6 to 6
- depth: int32 [32], P('genome'), may hold values from 1 to 4
Outputs:
- ld_effects: float32 [8192, 512], P('genome', 'samp')
The draws below stay inside these ranges and needn't reach their ends.
Inputs may be any that keep to these rules, and one draw needn't show every extreme that they name: Every block's window depth lies between 1 and 4.
All inputs are finite; a program needn't handle non-finite values.
Results may differ from the reference program's by a relative error of at most 0.0029.
Values may be sent and summed in bfloat16 or wider, within the bound.
A program may use at most 128 MiB of HBM per device.

```python
import jax
import jax.numpy as jnp
from jax import lax

BLK = 256
MAXDEPTH = 4
TRAITS = 512
SAMPLES = 16384
NBLOCKS = 32
VARIANTS = 8192


def plant(entries, own_key, least, largest):
    longest = entries.shape.index(max(entries.shape))
    spots = []
    for shift in (0, 1):
        where = [jax.random.randint(jax.random.fold_in(own_key, axis), (), 0, length) for axis, length in enumerate(entries.shape)]
        where[longest] = (where[longest] + shift) % entries.shape[longest]
        spots.append(tuple(where))
    return entries.at[spots[0]].set(least).at[spots[1]].set(largest)


def block_scale(own_key, extent, shards, smallest, largest):
    loudness = 1.0
    for position, blocks in shards:
        draws = jax.random.uniform(jax.random.fold_in(jax.random.fold_in(own_key, 6), position), (blocks,), jnp.float32, smallest / len(shards), largest / len(shards))
        loudness = loudness * jnp.repeat(jnp.exp(draws), extent[position] // blocks).reshape((-1,) + (1,) * (len(extent) - 1 - position))
    return loudness


def scatter_about(stream_key, shape, spread, bound, split=(), kind=jnp.bfloat16):
    entries = spread * jax.random.normal(stream_key, shape, jnp.float32)
    if split:
        entries = entries * block_scale(stream_key, shape, split, -0.22, 0.18)
    return jnp.clip(entries, -bound, bound).astype(kind)


def setup_inputs(seed: int = 0) -> dict:
    arg_keys = jax.random.split(jax.random.key(seed), 4)
    return {
        "dosage": scatter_about(arg_keys[0], (SAMPLES, VARIANTS), 1.0, 6.0, ((0, 4), (1, 8))),
        "effects": scatter_about(arg_keys[1], (VARIANTS, TRAITS), 1.0, 6.0, ((0, 8), (1, 4))),
        "depth": plant(jax.random.randint(arg_keys[2], (NBLOCKS,), 1, 5), jax.random.fold_in(arg_keys[2], 1), 1, 4).astype(jnp.int32),
    }


def reference(dosage, effects, depth):
    span = MAXDEPTH + 1
    padded_x = jnp.pad(dosage, ((0, 0), (0, MAXDEPTH * BLK)))
    padded_b = jnp.pad(effects, ((0, MAXDEPTH * BLK), (0, 0)))
    column_block = jnp.arange(span * BLK, dtype=jnp.int32) // BLK

    def one_block(index):
        start = (index * BLK).astype(jnp.int32)
        own_x = lax.dynamic_slice_in_dim(dosage, start, BLK, 1)
        window_x = lax.dynamic_slice_in_dim(padded_x, start, span * BLK, 1)
        gram = lax.dot_general(own_x, window_x, (((0,), (0,)), ((), ())), preferred_element_type=jnp.float32)
        gram = gram / jnp.float32(SAMPLES)
        keep = (column_block <= depth[index]).astype(jnp.float32)
        corr = (gram * keep[None, :]).astype(jnp.bfloat16)
        window_b = lax.dynamic_slice_in_dim(padded_b, start, span * BLK, 0)
        forward = jnp.dot(corr, window_b, preferred_element_type=jnp.float32)
        own_b = lax.dynamic_slice_in_dim(effects, start, BLK, 0)
        backward = lax.dot_general(corr[:, BLK:], own_b, (((0,), (0,)), ((), ())), preferred_element_type=jnp.float32)
        return forward, backward.reshape(MAXDEPTH, BLK, TRAITS)

    forward, backward = lax.map(one_block, jnp.arange(NBLOCKS, dtype=jnp.int32))
    total = forward
    for offset in range(1, span):
        moved = jnp.pad(backward[:, offset - 1], ((offset, 0), (0, 0), (0, 0)))[:NBLOCKS]
        total = total + moved
    return total.reshape(VARIANTS, TRAITS)
```

```python
import functools

import jax
import jax.numpy as jnp
from jax import lax
from jax.experimental import pallas as pl
from jax.experimental.pallas import tpu as pltpu
from jax.sharding import PartitionSpec as P

BLK = 256
MESH = pl.DeviceIdType.MESH
F32 = jnp.float32
BF16 = jnp.bfloat16
CONTRACT0 = (((0,), (0,)), ((), ()))
PARTS = (2, 4, 8, 8)


def gram(left, right):
    return lax.dot_general(left, right, CONTRACT0, preferred_element_type=F32)


def kernel(
    n_genome, n_samp, nb, half, traits, scale,
    x_ref, e_ref, depth_ref, out_ref,
    d_ref, own, xbuf, zbuf, gacc, eff, dep, loc, cro, par, far, lc_in, ly_out, ly_in, c_in, y_out, y_in, hop_out, hop_in,
    own_sem, own_e_sem, x_send, x_recv, z_send, z_recv, es_send, es_recv, ex_send, ex_recv,
    ds_send, ds_recv, lc_send, lc_recv, ly_send, ly_recv, c_send, c_recv, y_send, y_recv, h_send, h_recv,
):
    g = lax.axis_index("genome")
    s = lax.axis_index("samp")
    q = lax.rem(g, 2)
    sign = 1 - 2 * q
    partner = g + sign
    z_from = g + 2 * sign
    z_to = g - 2 * sign
    has_from = jnp.logical_and(z_from >= 0, z_from < n_genome)
    has_to = jnp.logical_and(z_to >= 0, z_to < n_genome)

    def mine(u):
        return u + q * (nb - 1 - 2 * u)

    def other(u):
        return nb - 1 - mine(u)

    core = lax.rem(s, 2)
    core_mate = s + 1 - 2 * core
    cross_mate = lax.rem(s + 2, n_samp)

    def cols(t):
        return pl.ds(pl.multiple_of(t * traits, traits), traits)

    my_cols = cols(s)
    keep_rows = pl.ds(pl.multiple_of(q * half, half), half)

    def remote(src, dst, ss, rsem, gg, sss):
        return pltpu.make_async_remote_copy(
            src_ref=src, dst_ref=dst, send_sem=ss, recv_sem=rsem,
            device_id=(gg, sss), device_id_type=MESH,
        )

    barrier = pltpu.get_barrier_semaphore()
    for mate in (core_mate, cross_mate):
        pl.semaphore_signal(barrier, inc=1, device_id=(g, mate), device_id_type=MESH)
    pl.semaphore_signal(barrier, inc=1, device_id=(partner, s), device_id_type=MESH)

    @pl.when(has_from)
    def _():
        pl.semaphore_signal(barrier, inc=1, device_id=(z_from, s), device_id_type=MESH)

    @pl.when(has_to)
    def _():
        pl.semaphore_signal(barrier, inc=1, device_id=(z_to, s), device_id_type=MESH)

    own_copies = [
        pltpu.make_async_copy(x_ref.at[:, b * BLK : (b + 1) * BLK], own.at[b], own_sem.at[b])
        for b in range(nb)
    ]
    own_e = pltpu.make_async_copy(e_ref, eff.at[0, :, my_cols], own_e_sem.at[0])
    own_e.start()
    for c in own_copies:
        c.start()
    pl.semaphore_wait(
        barrier, 3 + has_from.astype(jnp.int32) + has_to.astype(jnp.int32)
    )

    for b in range(nb):
        d_ref[b : b + 1, :] = jnp.full((1, BLK), depth_ref[b].astype(F32))

    def block_cols(b):
        return pl.ds(pl.multiple_of(b * BLK, BLK), BLK)

    last = nb - 1
    pieces = []
    for part in PARTS:
        low = pieces[-1][1] if pieces else 0
        pieces.append((low, low + half // part))

    def half_rows(which, low, high):
        return pl.ds(pl.multiple_of(which * half + low, 16), high - low)

    def x_part(t, low, high, n):
        return remote(
            x_ref.at[half_rows(1 - q, low, high), block_cols(other(t))], xbuf.at[t, low:high],
            x_send.at[n], x_recv.at[n], partner, s,
        )

    def z_part(t, low, high, n):
        return remote(
            x_ref.at[half_rows(q, low, high), block_cols(mine(t))], zbuf.at[t, low:high],
            z_send.at[n], z_recv.at[n], z_to, s,
        )

    x_copies = [x_part(t, 0, half, t) for t in range(last)]
    z_copies = [z_part(t, 0, half, t) for t in range(last)]
    x_last = [x_part(last, low, high, last + n) for n, (low, high) in enumerate(pieces)]
    z_last = [z_part(last, low, high, last + n) for n, (low, high) in enumerate(pieces)]
    d_x = remote(d_ref, dep.at[0], ds_send.at[0], ds_recv.at[0], partner, s)
    d_z = remote(d_ref, dep.at[1], ds_send.at[1], ds_recv.at[1], z_to, s)
    e_x = remote(e_ref, eff.at[1, :, my_cols], ex_send.at[0], ex_recv.at[0], partner, s)
    e_z = remote(e_ref, eff.at[2, :, my_cols], ex_send.at[1], ex_recv.at[1], z_to, s)
    d_x.start()
    e_x.start()
    for c in x_copies + x_last:
        c.start()

    @pl.when(has_to)
    def _():
        d_z.start()
        e_z.start()
        for c in z_copies + z_last:
            c.start()

    def gather(slot, source):
        across = cols(cross_mate)
        here = eff.at[slot, :, my_cols]
        there = eff.at[slot, :, across]
        return [
            remote(source, here, es_send.at[slot, 0], es_recv.at[slot, 0], g, core_mate),
            remote(source, here, es_send.at[slot, 1], es_recv.at[slot, 1], g, cross_mate),
            remote(there, there, es_send.at[slot, 2], es_recv.at[slot, 2], g, core_mate),
        ]

    e_own = gather(0, e_ref)
    e_partner = gather(1, eff.at[1, :, my_cols])
    e_far = gather(2, eff.at[2, :, my_cols])
    e_own[0].start()
    e_own[1].start()
    loc[...] = jnp.zeros_like(loc)
    cro[...] = jnp.zeros_like(cro)
    par[...] = jnp.zeros_like(par)
    far[...] = jnp.zeros_like(far)
    e_own[1].wait_recv()
    e_own[2].start()
    e_x.wait_recv()
    e_partner[0].start()
    e_partner[1].start()

    @pl.when(has_from)
    def _():
        e_z.wait_recv()
        e_far[0].start()
        e_far[1].start()

    own_e.wait()
    for c in own_copies:
        c.wait()
    e_own[0].wait_recv()
    e_own[2].wait_recv()

    def weight(drow, k):
        return jnp.where(drow >= k.astype(F32), F32(scale), F32(0.0))

    def rows(b):
        return pl.ds(pl.multiple_of(b * BLK, BLK), BLK)

    def local_row(i, carry):
        def local_pair(j, carry):
            full = gram(own[i, :half], own[j, :half]) + gram(own[i, half:], own[j, half:])
            full = full * weight(d_ref[pl.ds(i, 1), :], j - i)
            high = full.astype(BF16)
            low = (full - high.astype(F32)).astype(BF16)
            ej = eff[0, rows(j), :]
            loc[rows(i), :] += jnp.dot(high, ej, preferred_element_type=F32) + jnp.dot(
                low, ej, preferred_element_type=F32
            )

            @pl.when(j > i)
            def _():
                ei = eff[0, rows(i), :]
                loc[rows(j), :] += gram(high, ei) + gram(low, ei)

            return carry

        return lax.fori_loop(i, nb, local_pair, carry)

    lax.fori_loop(0, nb, local_row, 0)
    def loc_core(y):
        return remote(
            loc.at[:, cols(2 * y + 1 - core)], lc_in.at[y], lc_send.at[y], lc_recv.at[y], g, core_mate
        )

    loc_across = remote(ly_out, ly_in, ly_send.at[0], ly_recv.at[0], g, cross_mate)
    loc_core(0).start()
    loc_core(1).start()
    e_partner[1].wait_recv()
    e_partner[2].start()
    d_x.wait_recv()

    @pl.when(has_from)
    def _():
        e_far[1].wait_recv()
        e_far[2].start()
        d_z.wait_recv()

    my_y = s // 2
    mate_y = 1 - my_y
    loc_core(0).wait_recv()
    loc_core(1).wait_recv()
    ly_out[...] = loc[:, cols(cross_mate)] + lc_in[mate_y]
    loc_across.start()
    e_partner[0].wait_recv()
    e_partner[2].wait_recv()

    @pl.when(has_from)
    def _():
        e_far[0].wait_recv()
        e_far[2].wait_recv()

    kinds = {"own": (0, cro), "partner": (1, par), "far": (2, far)}

    def block_rows(t):
        return pl.ds(t * BLK, BLK)

    def to_core(kind, t):
        n, acc = kinds[kind]
        return [
            remote(
                acc.at[block_rows(t), cols(2 * y + 1 - core)], c_in.at[n, t, y],
                c_send.at[n, t, y], c_recv.at[n, t, y], g, core_mate,
            )
            for y in range(2)
        ]

    def across(kind, t):
        n, _ = kinds[kind]
        return remote(y_out.at[n, t], y_in.at[n, t], y_send.at[n, t], y_recv.at[n, t], g, cross_mate)

    def publish(kind, t):
        for c in to_core(kind, t):
            c.start()

    def relay(kind, t):
        n, acc = kinds[kind]
        for c in to_core(kind, t):
            c.wait_recv()
        y_out[n, t] = (acc[block_rows(t), cols(cross_mate)] + c_in[n, t, mate_y]).astype(BF16)
        across(kind, t).start()

    def collect(kind, t):
        n, acc = kinds[kind]
        across(kind, t).wait_recv()
        return acc[block_rows(t), my_cols] + c_in[n, t, my_y] + y_in[n, t].astype(F32)

    def hop(n, t):
        return remote(
            hop_out.at[n, t], hop_in.at[n, t], h_send.at[n, t], h_recv.at[n, t],
            partner if n == 0 else z_from, s,
        )

    def prepare(n, t):
        hop_out[n, t] = collect("partner" if n == 0 else "far", t).astype(BF16)

    def forward(n, t):
        prepare(n, t)
        hop(n, t).start()

    def x_weight(t, u):
        mu, mt = mine(u), mine(t)
        drow = jnp.where(q == 0, d_ref[pl.ds(mu, 1), :], dep[0, pl.ds(mt, 1), :])
        return weight(drow, jnp.int32(nb) + t - u)

    def x_apply(t, u, full):
        high = full.astype(BF16)
        cro[rows(u), :] += jnp.dot(high, eff[1, rows(other(nb - 1 - t)), :], preferred_element_type=F32)
        par[t * BLK : (t + 1) * BLK, :] += gram(high, eff[0, rows(mine(u)), :])

    def z_weight(t, v):
        mt, mv = mine(t), mine(v)
        drow = jnp.where(q == 0, dep[0, pl.ds(mt, 1), :], dep[1, pl.ds(mv, 1), :])
        return weight(drow, jnp.int32(nb) + v - t)

    def z_apply(t, v, full):
        high = full.astype(BF16)
        par[t * BLK : (t + 1) * BLK, :] += jnp.dot(high, eff[2, rows(mine(v)), :], preferred_element_type=F32)
        far[rows(v), :] += gram(high, eff[1, rows(mine(t)), :])

    for t in range(last):
        x_copies[t].wait_recv()

        def x_pair(u, carry):
            x_apply(t, u, gram(own[mine(u), keep_rows, :], xbuf[t]) * x_weight(t, u))
            return carry

        @pl.when(has_from)
        def _():
            z_copies[t].wait_recv()

            def z_pair(v, carry):
                z_apply(t, v, gram(xbuf[t], zbuf[v]) * z_weight(t, v))
                return carry

            lax.fori_loop(0, t + 1, z_pair, 0)

        lax.fori_loop(t, nb, x_pair, 0)
        publish("partner", t)
        publish("own", t)
        if t == 0:
            loc_across.wait_recv()
            out_ref[...] = loc[:, my_cols] + lc_in[my_y] + ly_in[...]
        relay("partner", t)
        relay("own", t)
        prepare(0, t)
        out_ref[rows(mine(t)), :] += collect("own", t)

    for n, (low, high) in enumerate(pieces):
        final = n == len(pieces) - 1
        x_last[n].wait_recv()
        if final:
            for t in range(last):
                hop(0, t).start()
        mu = mine(jnp.int32(last))
        x_piece = xbuf[last, low:high]
        full = gram(own[mu, half_rows(q, low, high), :], x_piece)
        if n:
            full = gacc[nb] + full
        if final:
            x_apply(last, jnp.int32(last), full * x_weight(last, jnp.int32(last)))
        else:
            gacc[nb] = full

        @pl.when(has_from)
        def _():
            for v in range(nb):
                if v == last:
                    z_last[n].wait_recv()
                full = gram(xbuf[last, low:high], zbuf[v, low:high])
                if n:
                    full = gacc[v] + full
                if final:
                    z_apply(last, jnp.int32(v), full * z_weight(last, jnp.int32(v)))
                    publish("far", v)
                    if v > 0:
                        relay("far", v - 1)
                else:
                    gacc[v] = full

    publish("partner", last)
    publish("own", last)

    @pl.when(has_from)
    def _():
        relay("far", last)

    relay("partner", last)
    relay("own", last)

    @pl.when(has_from)
    def _():
        for v in range(nb):
            forward(1, v)

    forward(0, last)
    for t in range(last):
        hop(0, t).wait_recv()
        out_ref[rows(other(t)), :] += hop_in[0, t].astype(F32)
    out_ref[rows(mine(last)), :] += collect("own", last)

    @pl.when(has_to)
    def _():
        for v in range(nb):
            hop(1, v).wait_recv()
            out_ref[rows(mine(v)), :] += hop_in[1, v].astype(F32)

    hop(0, last).wait_recv()
    out_ref[rows(other(last)), :] += hop_in[0, last].astype(F32)

    d_x.wait_send()
    e_x.wait_send()
    for c in x_copies + x_last:
        c.wait_send()

    @pl.when(has_to)
    def _():
        d_z.wait_send()
        e_z.wait_send()
        for c in z_copies + z_last:
            c.wait_send()

    for c in e_own + e_partner + [loc_core(0), loc_core(1), loc_across]:
        c.wait_send()
    for t in range(nb):
        for kind in ("own", "partner"):
            for c in to_core(kind, t) + [across(kind, t)]:
                c.wait_send()
        hop(0, t).wait_send()

    @pl.when(has_from)
    def _():
        for c in e_far:
            c.wait_send()
        for t in range(nb):
            for c in to_core("far", t) + [across("far", t)]:
                c.wait_send()
            hop(1, t).wait_send()


def body(n_genome, n_samp, dosage, effects, depth):
    nb = depth.shape[0]
    samples, variants = dosage.shape
    traits = effects.shape[1]
    all_traits = traits * n_samp
    half = samples // 2
    dma = pltpu.SemaphoreType.DMA
    return pl.pallas_call(
        functools.partial(kernel, n_genome, n_samp, nb, half, traits, 1.0 / (samples * n_samp)),
        out_shape=jax.ShapeDtypeStruct((variants, traits), F32),
        in_specs=[
            pl.BlockSpec(memory_space=pl.ANY),
            pl.BlockSpec(memory_space=pl.ANY),
            pl.BlockSpec(memory_space=pltpu.SMEM),
        ],
        out_specs=pl.BlockSpec(memory_space=pltpu.VMEM),
        scratch_shapes=[
            pltpu.VMEM((8, BLK), F32),
            pltpu.VMEM((nb, samples, BLK), BF16),
            pltpu.VMEM((nb, half, BLK), BF16),
            pltpu.VMEM((nb, half, BLK), BF16),
            pltpu.VMEM((nb + 1, BLK, BLK), F32),
            pltpu.VMEM((3, variants, all_traits), BF16),
            pltpu.VMEM((2, 8, BLK), F32),
            pltpu.VMEM((variants, all_traits), F32),
            pltpu.VMEM((variants, all_traits), F32),
            pltpu.VMEM((variants, all_traits), F32),
            pltpu.VMEM((variants, all_traits), F32),
            pltpu.VMEM((2, variants, traits), F32),
            pltpu.VMEM((variants, traits), F32),
            pltpu.VMEM((variants, traits), F32),
            pltpu.VMEM((3, nb, 2, BLK, traits), F32),
            pltpu.VMEM((3, nb, BLK, traits), BF16),
            pltpu.VMEM((3, nb, BLK, traits), BF16),
            pltpu.VMEM((2, nb, BLK, traits), BF16),
            pltpu.VMEM((2, nb, BLK, traits), BF16),
            dma((nb,)), dma((1,)),
            dma((nb - 1 + len(PARTS),)), dma((nb - 1 + len(PARTS),)),
            dma((nb - 1 + len(PARTS),)), dma((nb - 1 + len(PARTS),)),
            dma((3, 3)), dma((3, 3)),
            dma((2,)), dma((2,)), dma((2,)), dma((2,)),
            dma((2,)), dma((2,)), dma((1,)), dma((1,)),
            dma((3, nb, 2)), dma((3, nb, 2)), dma((3, nb)), dma((3, nb)),
            dma((2, nb)), dma((2, nb)),
        ],
        compiler_params=pltpu.CompilerParams(
            collective_id=0, has_side_effects=True, vmem_limit_bytes=60 * 1024 * 1024
        ),
        cost_estimate=pl.CostEstimate(
            flops=2 * 20 * BLK * BLK * samples, bytes_accessed=4 * samples * variants, transcendentals=0
        ),
    )(dosage, effects, depth)


def solution(mesh):
    return jax.shard_map(
        functools.partial(body, mesh.shape["genome"], mesh.shape["samp"]),
        mesh=mesh,
        in_specs=(P("samp", "genome"), P("genome", "samp"), P("genome")),
        out_specs=P("genome", "samp"),
        check_vma=False,
    )
```

```python
import functools

import jax
import jax.numpy as jnp
from jax import lax
from jax.experimental import pallas as pl
from jax.experimental.pallas import tpu as pltpu
from jax.sharding import PartitionSpec as P

BLK = 256
MESH = pl.DeviceIdType.MESH
F32 = jnp.float32
BF16 = jnp.bfloat16
CONTRACT0 = (((0,), (0,)), ((), ()))
PARTS = (2, 4, 8, 8)


def gram(left, right):
    return lax.dot_general(left, right, CONTRACT0, preferred_element_type=F32)


def kernel(
    n_genome, n_samp, nb, half, traits, scale,
    x_ref, e_ref, depth_ref, out_ref,
    d_ref, own, xbuf, zbuf, gacc, eff, dep, loc, cro, par, far, lc_in, ly_out, ly_in, c_in, y_out, y_in, hop_out, hop_in,
    own_sem, own_e_sem, x_send, x_recv, z_send, z_recv, es_send, es_recv, ex_send, ex_recv,
    ds_send, ds_recv, lc_send, lc_recv, ly_send, ly_recv, c_send, c_recv, y_send, y_recv, h_send, h_recv,
):
    g = lax.axis_index("genome")
    s = lax.axis_index("samp")
    q = lax.rem(g, 2)
    sign = 1 - 2 * q
    partner = g + sign
    z_from = g + 2 * sign
    z_to = g - 2 * sign
    has_from = jnp.logical_and(z_from >= 0, z_from < n_genome)
    has_to = jnp.logical_and(z_to >= 0, z_to < n_genome)

    def mine(u):
        return u + q * (nb - 1 - 2 * u)

    def other(u):
        return nb - 1 - mine(u)

    core = lax.rem(s, 2)
    core_mate = s + 1 - 2 * core
    cross_mate = lax.rem(s + 2, n_samp)

    def cols(t):
        return pl.ds(pl.multiple_of(t * traits, traits), traits)

    my_cols = cols(s)
    keep_rows = pl.ds(pl.multiple_of(q * half, half), half)

    def remote(src, dst, ss, rsem, gg, sss):
        return pltpu.make_async_remote_copy(
            src_ref=src, dst_ref=dst, send_sem=ss, recv_sem=rsem,
            device_id=(gg, sss), device_id_type=MESH,
        )

    barrier = pltpu.get_barrier_semaphore()
    for mate in (core_mate, cross_mate):
        pl.semaphore_signal(barrier, inc=1, device_id=(g, mate), device_id_type=MESH)
    pl.semaphore_signal(barrier, inc=1, device_id=(partner, s), device_id_type=MESH)

    @pl.when(has_from)
    def _():
        pl.semaphore_signal(barrier, inc=1, device_id=(z_from, s), device_id_type=MESH)

    @pl.when(has_to)
    def _():
        pl.semaphore_signal(barrier, inc=1, device_id=(z_to, s), device_id_type=MESH)

    own_copies = [
        pltpu.make_async_copy(x_ref.at[:, b * BLK : (b + 1) * BLK], own.at[b], own_sem.at[b])
        for b in range(nb)
    ]
    own_e = pltpu.make_async_copy(e_ref, eff.at[0, :, my_cols], own_e_sem.at[0])
    own_e.start()
    for c in own_copies:
        c.start()
    pl.semaphore_wait(
        barrier, 3 + has_from.astype(jnp.int32) + has_to.astype(jnp.int32)
    )

    for b in range(nb):
        d_ref[b : b + 1, :] = jnp.full((1, BLK), depth_ref[b].astype(F32))

    def block_cols(b):
        return pl.ds(pl.multiple_of(b * BLK, BLK), BLK)

    last = nb - 1
    pieces = []
    for part in PARTS:
        low = pieces[-1][1] if pieces else 0
        pieces.append((low, low + half // part))

    def half_rows(which, low, high):
        return pl.ds(pl.multiple_of(which * half + low, 16), high - low)

    def x_part(t, low, high, n):
        return remote(
            x_ref.at[half_rows(1 - q, low, high), block_cols(other(t))], xbuf.at[t, low:high],
            x_send.at[n], x_recv.at[n], partner, s,
        )

    def z_part(t, low, high, n):
        return remote(
            x_ref.at[half_rows(q, low, high), block_cols(mine(t))], zbuf.at[t, low:high],
            z_send.at[n], z_recv.at[n], z_to, s,
        )

    x_copies = [x_part(t, 0, half, t) for t in range(last)]
    z_copies = [z_part(t, 0, half, t) for t in range(last)]
    x_last = [x_part(last, low, high, last + n) for n, (low, high) in enumerate(pieces)]
    z_last = [z_part(last, low, high, last + n) for n, (low, high) in enumerate(pieces)]
    d_x = remote(d_ref, dep.at[0], ds_send.at[0], ds_recv.at[0], partner, s)
    d_z = remote(d_ref, dep.at[1], ds_send.at[1], ds_recv.at[1], z_to, s)
    e_x = remote(e_ref, eff.at[1, :, my_cols], ex_send.at[0], ex_recv.at[0], partner, s)
    e_z = remote(e_ref, eff.at[2, :, my_cols], ex_send.at[1], ex_recv.at[1], z_to, s)
    d_x.start()
    e_x.start()
    for c in x_copies + x_last:
        c.start()

    @pl.when(has_to)
    def _():
        d_z.start()
        e_z.start()
        for c in z_copies + z_last:
            c.start()

    def gather(slot, source):
        across = cols(cross_mate)
        here = eff.at[slot, :, my_cols]
        there = eff.at[slot, :, across]
        return [
            remote(source, here, es_send.at[slot, 0], es_recv.at[slot, 0], g, core_mate),
            remote(source, here, es_send.at[slot, 1], es_recv.at[slot, 1], g, cross_mate),
            remote(there, there, es_send.at[slot, 2], es_recv.at[slot, 2], g, core_mate),
        ]

    e_own = gather(0, e_ref)
    e_partner = gather(1, eff.at[1, :, my_cols])
    e_far = gather(2, eff.at[2, :, my_cols])
    e_own[0].start()
    e_own[1].start()
    loc[...] = jnp.zeros_like(loc)
    cro[...] = jnp.zeros_like(cro)
    par[...] = jnp.zeros_like(par)
    far[...] = jnp.zeros_like(far)
    e_own[1].wait_recv()
    e_own[2].start()
    e_x.wait_recv()
    e_partner[0].start()
    e_partner[1].start()

    @pl.when(has_from)
    def _():
        e_z.wait_recv()
        e_far[0].start()
        e_far[1].start()

    own_e.wait()
    for c in own_copies:
        c.wait()
    e_own[0].wait_recv()
    e_own[2].wait_recv()

    def weight(drow, k):
        return jnp.where(drow >= k.astype(F32), F32(scale), F32(0.0))

    def rows(b):
        return pl.ds(pl.multiple_of(b * BLK, BLK), BLK)

    def local_row(i, carry):
        def local_pair(j, carry):
            full = gram(own[i, :half], own[j, :half]) + gram(own[i, half:], own[j, half:])
            full = full * weight(d_ref[pl.ds(i, 1), :], j - i)
            high = full.astype(BF16)
            low = (full - high.astype(F32)).astype(BF16)
            ej = eff[0, rows(j), :]
            loc[rows(i), :] += jnp.dot(high, ej, preferred_element_type=F32) + jnp.dot(
                low, ej, preferred_element_type=F32
            )

            @pl.when(j > i)
            def _():
                ei = eff[0, rows(i), :]
                loc[rows(j), :] += gram(high, ei) + gram(low, ei)

            return carry

        return lax.fori_loop(i, nb, local_pair, carry)

    lax.fori_loop(0, nb, local_row, 0)
    def loc_core(y):
        return remote(
            loc.at[:, cols(2 * y + 1 - core)], lc_in.at[y], lc_send.at[y], lc_recv.at[y], g, core_mate
        )

    loc_across = remote(ly_out, ly_in, ly_send.at[0], ly_recv.at[0], g, cross_mate)
    loc_core(0).start()
    loc_core(1).start()
    e_partner[1].wait_recv()
    e_partner[2].start()
    d_x.wait_recv()

    @pl.when(has_from)
    def _():
        e_far[1].wait_recv()
        e_far[2].start()
        d_z.wait_recv()

    my_y = s // 2
    mate_y = 1 - my_y
    loc_core(0).wait_recv()
    loc_core(1).wait_recv()
    ly_out[...] = loc[:, cols(cross_mate)] + lc_in[mate_y]
    loc_across.start()
    e_partner[0].wait_recv()
    e_partner[2].wait_recv()

    @pl.when(has_from)
    def _():
        e_far[0].wait_recv()
        e_far[2].wait_recv()

    kinds = {"own": (0, cro), "partner": (1, par), "far": (2, far)}

    def block_rows(t):
        return pl.ds(t * BLK, BLK)

    def to_core(kind, t):
        n, acc = kinds[kind]
        return [
            remote(
                acc.at[block_rows(t), cols(2 * y + 1 - core)], c_in.at[n, t, y],
                c_send.at[n, t, y], c_recv.at[n, t, y], g, core_mate,
            )
            for y in range(2)
        ]

    def across(kind, t):
        n, _ = kinds[kind]
        return remote(y_out.at[n, t], y_in.at[n, t], y_send.at[n, t], y_recv.at[n, t], g, cross_mate)

    def publish(kind, t):
        for c in to_core(kind, t):
            c.start()

    def relay(kind, t):
        n, acc = kinds[kind]
        for c in to_core(kind, t):
            c.wait_recv()
        y_out[n, t] = (acc[block_rows(t), cols(cross_mate)] + c_in[n, t, mate_y]).astype(BF16)
        across(kind, t).start()

    def collect(kind, t):
        n, acc = kinds[kind]
        across(kind, t).wait_recv()
        return acc[block_rows(t), my_cols] + c_in[n, t, my_y] + y_in[n, t].astype(F32)

    def hop(n, t):
        return remote(
            hop_out.at[n, t], hop_in.at[n, t], h_send.at[n, t], h_recv.at[n, t],
            partner if n == 0 else z_from, s,
        )

    def prepare(n, t):
        hop_out[n, t] = collect("partner" if n == 0 else "far", t).astype(BF16)

    def forward(n, t):
        prepare(n, t)
        hop(n, t).start()

    def x_weight(t, u):
        mu, mt = mine(u), mine(t)
        drow = jnp.where(q == 0, d_ref[pl.ds(mu, 1), :], dep[0, pl.ds(mt, 1), :])
        return weight(drow, jnp.int32(nb) + t - u)

    def x_apply(t, u, full):
        high = full.astype(BF16)
        cro[rows(u), :] += jnp.dot(high, eff[1, rows(other(nb - 1 - t)), :], preferred_element_type=F32)
        par[t * BLK : (t + 1) * BLK, :] += gram(high, eff[0, rows(mine(u)), :])

    def z_weight(t, v):
        mt, mv = mine(t), mine(v)
        drow = jnp.where(q == 0, dep[0, pl.ds(mt, 1), :], dep[1, pl.ds(mv, 1), :])
        return weight(drow, jnp.int32(nb) + v - t)

    def z_apply(t, v, full):
        high = full.astype(BF16)
        par[t * BLK : (t + 1) * BLK, :] += jnp.dot(high, eff[2, rows(mine(v)), :], preferred_element_type=F32)
        far[rows(v), :] += gram(high, eff[1, rows(mine(t)), :])

    for t in range(last):
        x_copies[t].wait_recv()

        def x_pair(u, carry):
            x_apply(t, u, gram(own[mine(u), keep_rows, :], xbuf[t]) * x_weight(t, u))
            return carry

        @pl.when(has_from)
        def _():
            z_copies[t].wait_recv()

            def z_pair(v, carry):
                z_apply(t, v, gram(xbuf[t], zbuf[v]) * z_weight(t, v))
                return carry

            lax.fori_loop(0, t + 1, z_pair, 0)

        lax.fori_loop(t, nb, x_pair, 0)
        publish("partner", t)
        publish("own", t)
        if t == 0:
            loc_across.wait_recv()
            out_ref[...] = loc[:, my_cols] + lc_in[my_y] + ly_in[...]
        relay("partner", t)
        relay("own", t)
        prepare(0, t)
        out_ref[rows(mine(t)), :] += collect("own", t)

    for n, (low, high) in enumerate(pieces):
        final = n == len(pieces) - 1
        x_last[n].wait_recv()
        if final:
            for t in range(last):
                hop(0, t).start()
        mu = mine(jnp.int32(last))
        x_piece = xbuf[last, low:high]
        full = gram(own[mu, half_rows(q, low, high), :], x_piece)
        if n:
            full = gacc[nb] + full
        if final:
            x_apply(last, jnp.int32(last), full * x_weight(last, jnp.int32(last)))
        else:
            gacc[nb] = full

        @pl.when(has_from)
        def _():
            for v in range(nb):
                if v == last:
                    z_last[n].wait_recv()
                full = gram(xbuf[last, low:high], zbuf[v, low:high])
                if n:
                    full = gacc[v] + full
                if final:
                    z_apply(last, jnp.int32(v), full * z_weight(last, jnp.int32(v)))
                    publish("far", v)
                    if v > 0:
                        relay("far", v - 1)
                else:
                    gacc[v] = full

    publish("partner", last)
    publish("own", last)

    @pl.when(has_from)
    def _():
        relay("far", last)

    relay("partner", last)
    relay("own", last)

    @pl.when(has_from)
    def _():
        for v in range(nb):
            forward(1, v)

    forward(0, last)
    for t in range(last):
        hop(0, t).wait_recv()
        out_ref[rows(other(t)), :] += hop_in[0, t].astype(F32)
    out_ref[rows(mine(last)), :] += collect("own", last)

    @pl.when(has_to)
    def _():
        for v in range(nb):
            hop(1, v).wait_recv()
            out_ref[rows(mine(v)), :] += hop_in[1, v].astype(F32)

    hop(0, last).wait_recv()
    out_ref[rows(other(last)), :] += hop_in[0, last].astype(F32)

    d_x.wait_send()
    e_x.wait_send()
    for c in x_copies + x_last:
        c.wait_send()

    @pl.when(has_to)
    def _():
        d_z.wait_send()
        e_z.wait_send()
        for c in z_copies + z_last:
            c.wait_send()

    for c in e_own + e_partner + [loc_core(0), loc_core(1), loc_across]:
        c.wait_send()
    for t in range(nb):
        for kind in ("own", "partner"):
            for c in to_core(kind, t) + [across(kind, t)]:
                c.wait_send()
        hop(0, t).wait_send()

    @pl.when(has_from)
    def _():
        for c in e_far:
            c.wait_send()
        for t in range(nb):
            for c in to_core("far", t) + [across("far", t)]:
                c.wait_send()
            hop(1, t).wait_send()


def body(n_genome, n_samp, dosage, effects, depth):
    nb = depth.shape[0]
    samples, variants = dosage.shape
    traits = effects.shape[1]
    all_traits = traits * n_samp
    half = samples // 2
    dma = pltpu.SemaphoreType.DMA
    return pl.pallas_call(
        functools.partial(kernel, n_genome, n_samp, nb, half, traits, 1.0 / (samples * n_samp)),
        out_shape=pltpu.VMEM((variants, traits), F32),
        in_specs=[
            pl.BlockSpec(memory_space=pl.ANY),
            pl.BlockSpec(memory_space=pl.ANY),
            pl.BlockSpec(memory_space=pltpu.SMEM),
        ],
        out_specs=pl.BlockSpec(memory_space=pltpu.VMEM),
        scratch_shapes=[
            pltpu.VMEM((8, BLK), F32),
            pltpu.VMEM((nb, samples, BLK), BF16),
            pltpu.VMEM((nb, half, BLK), BF16),
            pltpu.VMEM((nb, half, BLK), BF16),
            pltpu.VMEM((nb + 1, BLK, BLK), F32),
            pltpu.VMEM((3, variants, all_traits), BF16),
            pltpu.VMEM((2, 8, BLK), F32),
            pltpu.VMEM((variants, all_traits), F32),
            pltpu.VMEM((variants, all_traits), F32),
            pltpu.VMEM((variants, all_traits), F32),
            pltpu.VMEM((variants, all_traits), F32),
            pltpu.VMEM((2, variants, traits), F32),
            pltpu.VMEM((variants, traits), F32),
            pltpu.VMEM((variants, traits), F32),
            pltpu.VMEM((3, nb, 2, BLK, traits), F32),
            pltpu.VMEM((3, nb, BLK, traits), BF16),
            pltpu.VMEM((3, nb, BLK, traits), BF16),
            pltpu.VMEM((2, nb, BLK, traits), BF16),
            pltpu.VMEM((2, nb, BLK, traits), BF16),
            dma((nb,)), dma((1,)),
            dma((nb - 1 + len(PARTS),)), dma((nb - 1 + len(PARTS),)),
            dma((nb - 1 + len(PARTS),)), dma((nb - 1 + len(PARTS),)),
            dma((3, 3)), dma((3, 3)),
            dma((2,)), dma((2,)), dma((2,)), dma((2,)),
            dma((2,)), dma((2,)), dma((1,)), dma((1,)),
            dma((3, nb, 2)), dma((3, nb, 2)), dma((3, nb)), dma((3, nb)),
            dma((2, nb)), dma((2, nb)),
        ],
        compiler_params=pltpu.CompilerParams(
            collective_id=0, has_side_effects=True, vmem_limit_bytes=60 * 1024 * 1024
        ),
        cost_estimate=pl.CostEstimate(
            flops=2 * 20 * BLK * BLK * samples, bytes_accessed=4 * samples * variants, transcendentals=0
        ),
    )(dosage, effects, depth)


def solution(mesh):
    return jax.shard_map(
        functools.partial(body, mesh.shape["genome"], mesh.shape["samp"]),
        mesh=mesh,
        in_specs=(P("samp", "genome"), P("genome", "samp"), P("genome")),
        out_specs=P("genome", "samp"),
        check_vma=False,
    )
```

```python
import functools

import jax
import jax.numpy as jnp
from jax import lax
from jax.experimental import pallas as pl
from jax.experimental.pallas import tpu as pltpu
from jax.sharding import PartitionSpec as P

BLK = 256
HB = BLK // 2
MESH = pl.DeviceIdType.MESH
F32 = jnp.float32
BF16 = jnp.bfloat16
CONTRACT0 = (((0,), (0,)), ((), ()))
PARTS = (2, 4, 8, 8)


def gram(left, right):
    return lax.dot_general(left, right, CONTRACT0, preferred_element_type=F32)


def dot(left, right):
    return jnp.dot(left, right, preferred_element_type=F32)


def make_groups(nb):
    last = nb - 1
    split = last * BLK + HB
    x = [(t, nb, t * BLK, (t + 1) * BLK) for t in range(last)]
    x += [(last, nb, last * BLK, split), (last, nb, split, nb * BLK)]
    z = [(0, t + 1, t * BLK, (t + 1) * BLK) for t in range(last)]
    z += [(0, last, last * BLK, split)]
    z += [(v, v + 1, split, nb * BLK) for v in range(last)] + [(last, nb, last * BLK, nb * BLK)]
    return x, z


def kernel(
    n_genome, n_samp, nb, half, scale,
    x_ref, e_ref, depth_ref, out_ref,
    d_ref, dep, own, xbuf, zbuf, eff,
    sum_x, sum_z, sum_l, cin_x, cin_z, cin_l, yo_x, yo_z, yo_l, yi_x, yi_z, yi_l, cor_x, cor_z, cor_l,
    acc, par, far, hop_out, hop_in,
    own_sem, own_e_sem, x_send, x_recv, z_send, z_recv, ex_send, ex_recv, ez_send, ez_recv, ds_send, ds_recv,
    a_send, a_recv, b_send, b_recv, c_send, c_recv, h_send, h_recv,
):
    g = lax.axis_index("genome")
    s = lax.axis_index("samp")
    q = lax.rem(g, 2)
    sign = 1 - 2 * q
    partner = g + sign
    z_from = g + 2 * sign
    z_to = g - 2 * sign
    has_from = jnp.logical_and(z_from >= 0, z_from < n_genome)
    has_to = jnp.logical_and(z_to >= 0, z_to < n_genome)
    last = nb - 1
    split = last * BLK + HB

    def mine(u):
        return u + q * (nb - 1 - 2 * u)

    def other(u):
        return nb - 1 - mine(u)

    core = lax.rem(s, 2)
    core_mate = s + 1 - 2 * core
    cross_mate = lax.rem(s + 2, n_samp)

    def remote(src, dst, ss, rsem, gg, sss):
        return pltpu.make_async_remote_copy(
            src_ref=src, dst_ref=dst, send_sem=ss, recv_sem=rsem,
            device_id=(gg, sss), device_id_type=MESH,
        )

    def at_block(b):
        return pl.ds(pl.multiple_of(b * BLK, BLK), BLK)

    def half_rows(which, low, high):
        return pl.ds(pl.multiple_of(which * half + low, 16), high - low)

    barrier = pltpu.get_barrier_semaphore()
    for mate in (core_mate, cross_mate):
        pl.semaphore_signal(barrier, inc=1, device_id=(g, mate), device_id_type=MESH)
    pl.semaphore_signal(barrier, inc=1, device_id=(partner, s), device_id_type=MESH)

    @pl.when(has_from)
    def _():
        pl.semaphore_signal(barrier, inc=1, device_id=(z_from, s), device_id_type=MESH)

    @pl.when(has_to)
    def _():
        pl.semaphore_signal(barrier, inc=1, device_id=(z_to, s), device_id_type=MESH)

    own_copies = [
        pltpu.make_async_copy(x_ref.at[:, at_block(mine(u))], own.at[u], own_sem.at[u]) for u in range(nb)
    ]
    own_effects = [
        pltpu.make_async_copy(e_ref.at[at_block(mine(u)), :], eff.at[0, u * BLK : (u + 1) * BLK], own_e_sem.at[u])
        for u in range(nb)
    ]
    for c in own_copies + own_effects:
        c.start()
    for u in range(nb):
        d_ref[u : u + 1, :] = jnp.full((1, BLK), depth_ref[mine(u)].astype(F32))
    pl.semaphore_wait(
        barrier, 3 + has_from.astype(jnp.int32) + has_to.astype(jnp.int32)
    )

    pieces = []
    for part in PARTS:
        low = pieces[-1][1] if pieces else 0
        pieces.append((low, low + half // part))

    def x_part(t, low, high, left, right, n):
        src = pl.ds(pl.multiple_of(other(t) * BLK + left, HB), right - left)
        return remote(
            x_ref.at[half_rows(1 - q, low, high), src], xbuf.at[t, low:high, left:right],
            x_send.at[n], x_recv.at[n], partner, s,
        )

    def z_part(t, low, high, n):
        return remote(
            x_ref.at[half_rows(q, low, high), at_block(mine(t))], zbuf.at[t, low:high],
            z_send.at[n], z_recv.at[n], z_to, s,
        )

    x_copies = [x_part(t, 0, half, 0, BLK, t) for t in range(last)] + [x_part(last, 0, half, 0, HB, last)]
    z_copies = [z_part(t, 0, half, t) for t in range(last)]
    x_last = [x_part(last, low, high, HB, BLK, nb + n) for n, (low, high) in enumerate(pieces)]
    z_last = [z_part(last, low, high, last + n) for n, (low, high) in enumerate(pieces)]
    e_x = [
        remote(e_ref.at[at_block(other(t)), :], eff.at[1, t * BLK : (t + 1) * BLK], ex_send.at[t], ex_recv.at[t], partner, s)
        for t in range(nb)
    ]
    e_z = [
        remote(e_ref.at[at_block(mine(v)), :], eff.at[2, v * BLK : (v + 1) * BLK], ez_send.at[v], ez_recv.at[v], z_to, s)
        for v in range(nb)
    ]
    d_x = remote(d_ref, dep.at[0], ds_send.at[0], ds_recv.at[0], partner, s)
    d_z = remote(d_ref, dep.at[1], ds_send.at[1], ds_recv.at[1], z_to, s)
    to_partner = [d_x] + x_copies + x_last + e_x
    to_next = [d_z] + z_copies + z_last + e_z
    for c in to_partner:
        c.start()

    @pl.when(has_to)
    def _():
        for c in to_next:
            c.start()

    groups_x, groups_z = make_groups(nb)
    n_x = len(groups_x)
    refs_x = (sum_x, cin_x, yo_x, yi_x, cor_x)
    refs_z = (sum_z, cin_z, yo_z, yi_z, cor_z)
    refs_l = (sum_l, cin_l, yo_l, yi_l, cor_l)
    X = [(i, refs_x) + gr for i, gr in enumerate(groups_x)]
    Z = [(n_x + i, refs_z) + gr for i, gr in enumerate(groups_z)]
    L = (n_x + len(groups_z), refs_l, 0, nb * (nb + 1) // 2, 0, BLK)

    def to_core(group):
        i, (total, cin, _, _, _), low, high, left, right = group
        return remote(
            total.at[low:high, 1 - core, :, left:right], cin.at[low:high, :, left:right],
            a_send.at[i], a_recv.at[i], g, core_mate,
        )

    def to_cross(group):
        i, (_, _, y_out, y_in, _), low, high, left, right = group
        return remote(
            y_out.at[low:high, :, left:right], y_in.at[low:high, :, left:right],
            b_send.at[i], b_recv.at[i], g, cross_mate,
        )

    def share(group):
        i, (_, _, _, _, corr), low, high, left, right = group
        part = corr.at[low:high, core, :, left:right]
        return remote(part, part, c_send.at[i], c_recv.at[i], g, core_mate)

    def stage1(group):
        to_core(group).start()

    def stage2(group):
        i, (total, cin, y_out, _, _), low, high, left, right = group
        to_core(group).wait_recv()
        for a in range(low, high):
            value = total[a, core, :, left:right] + cin[a, :, left:right]
            total[a, core, :, left:right] = value
            y_out[a, :, left:right] = value.astype(y_out.dtype)
        to_cross(group).start()

    def stage3(group):
        i, (total, _, _, y_in, corr), low, high, left, right = group
        to_cross(group).wait_recv()
        for a in range(low, high):
            value = total[a, core, :, left:right] + y_in[a, :, left:right].astype(F32)
            corr[a, core, :, left:right] = value.astype(BF16)
        share(group).start()

    def stage4(group):
        share(group).wait_recv()

    def weight(drow, k, width):
        return jnp.where(drow >= jnp.asarray(k, F32), F32(scale), F32(0.0))[:, :width]

    def row_of(ref, n):
        return ref[pl.ds(n, 1), :]

    def x_weight(t, u, width):
        drow = jnp.where(q == 0, row_of(d_ref, u), row_of(dep.at[0], nb - 1 - t))
        return weight(drow, (nb + t - u), width)

    def z_weight(t, v, width):
        drow = jnp.where(q == 0, row_of(dep.at[0], nb - 1 - t), row_of(dep.at[1], v))
        return weight(drow, (nb + v - t), width)

    def put(ref, a, left, right, value):
        for h in range(2):
            ref[a, h, :, left:right] = value[h * HB : (h + 1) * HB]

    def got(ref, a, left, right):
        return ref[a, :, :, left:right].reshape(BLK, right - left)

    def stack(ref, low, high, left, right):
        return ref[low:high, :, :, left:right].reshape((high - low) * BLK, right - left)

    def block(n):
        return slice(n * BLK, (n + 1) * BLK)

    for c in own_copies + own_effects:
        c.wait()

    def local_row(i, carry):
        def local_pair(j, carry):
            full = gram(own[i, :half], own[j, :half]) + gram(own[i, half:], own[j, half:])
            drow = jnp.where(q == 0, row_of(d_ref, i), row_of(d_ref, j))
            full = full * weight(drow, (j - i).astype(F32), BLK)
            put(sum_l, i * (2 * nb - i + 1) // 2 + (j - i), 0, BLK, full)
            return carry

        return lax.fori_loop(i, nb, local_pair, carry)

    lax.fori_loop(0, nb, local_row, 0)
    stage1(L)
    acc[...] = jnp.zeros_like(acc)
    stage2(L)
    d_x.wait_recv()

    @pl.when(has_from)
    def _():
        d_z.wait_recv()

    def x_grams(t, left, right):
        def pair(u, carry):
            full = gram(own[u, half_rows(q, 0, half), :], xbuf[t, :, left:right])
            put(sum_x, u, t * BLK + left, t * BLK + right, full * x_weight(t, u, right - left))
            return carry

        lax.fori_loop(t, nb, pair, 0)

    def z_grams(t, left, right, count):
        def pair(v, carry):
            full = gram(zbuf[v], xbuf[t, :, left:right])
            put(sum_z, v, t * BLK + left, t * BLK + right, full * z_weight(t, v, right - left))
            return carry

        lax.fori_loop(0, count, pair, 0)

    def local_products():
        def local_row(i, carry):
            def local_pair(j, carry):
                corr = got(cor_l, i * (2 * nb - i + 1) // 2 + (j - i), 0, BLK)
                acc[at_block(i), :] += dot(corr, eff[0, at_block(j), :])

                @pl.when(j > i)
                def _():
                    acc[at_block(j), :] += gram(corr, eff[0, at_block(i), :])

                return carry

            return lax.fori_loop(i, nb, local_pair, carry)

        lax.fori_loop(0, nb, local_row, 0)

    def both(stage, t):
        stage(X[t])

        @pl.when(has_from)
        def _():
            stage(Z[t])

    for t in range(nb):
        left, right = (0, BLK) if t < last else (0, HB)
        x_copies[t].wait_recv()
        x_grams(t, left, right)
        stage1(X[t])

        @pl.when(has_from)
        def _():
            if t < last:
                z_copies[t].wait_recv()
            z_grams(t, left, right, min(t + 1, last))
            stage1(Z[t])

        both(stage2, t)
        if t == 1:
            stage3(L)
            both(stage3, 0)
            stage4(L)
            local_products()
            both(stage4, 0)
        if t == 2:
            both(stage3, 1)
            both(stage4, 1)

    late_x = X[nb]
    late_z = Z[nb:]
    for n, (low, high) in enumerate(pieces):
        final = n == len(pieces) - 1

        def add(ref, a, left, right, value, factor):
            for h in range(2):
                part = value[h * HB : (h + 1) * HB]
                if n:
                    part = ref[a, h, :, left:right] + part
                ref[a, h, :, left:right] = part * factor if final else part

        if n == 1:
            both(stage3, 2)
        x_last[n].wait_recv()

        @pl.when(has_from)
        def _():
            for v in range(nb):
                if v == last:
                    z_last[n].wait_recv()
                left = HB if v < last else 0
                full = gram(zbuf[v, low:high], xbuf[last, low:high, left:])
                add(sum_z, v, last * BLK + left, nb * BLK, full, z_weight(last, v, BLK - left) if final else None)
                if final:
                    stage1(late_z[v])

        full = gram(own[last, half_rows(q, low, high), :], xbuf[last, low:high, HB:])
        add(sum_x, last, split, nb * BLK, full, x_weight(last, last, HB) if final else None)
        if final:
            stage1(late_x)

    @pl.when(has_from)
    def _():
        for v in range(nb):
            stage2(late_z[v])

    stage2(late_x)
    both(stage4, 2)
    both(stage3, last)

    def hop(n, t):
        return remote(
            hop_out.at[n, t], hop_in.at[n, t], h_send.at[n, t], h_recv.at[n, t],
            partner if n == 0 else z_from, s,
        )

    for t in range(last):
        par[block(t), :] = gram(stack(cor_x, t, nb, t * BLK, (t + 1) * BLK), eff[0, t * BLK :])
    both(stage4, last)
    par[last * BLK : split, :] = gram(got(cor_x, last, last * BLK, split), eff[0, block(last)])

    @pl.when(has_from)
    def _():
        for c in e_z:
            c.wait_recv()
        for t in range(last):
            par[block(t), :] += gram(stack(cor_z, 0, t + 1, t * BLK, (t + 1) * BLK), eff[2, : (t + 1) * BLK])

    for t in range(last):
        hop_out[0, t] = par[block(t), :].astype(BF16)
        hop(0, t).start()

    @pl.when(has_from)
    def _():
        stage3(late_z[0])
        stage3(late_z[1])
        par[last * BLK : split, :] += gram(stack(cor_z, 0, last, last * BLK, split), eff[2, : last * BLK])

    for c in e_x:
        c.wait_recv()

    @pl.when(has_from)
    def _():
        for v in range(last):
            far[block(v), :] = dot(got(cor_z, v, v * BLK, split), eff[1, v * BLK : split])
        for v in range(2, nb):
            stage3(late_z[v])

    stage3(late_x)

    @pl.when(has_from)
    def _():
        for v in range(nb):
            stage4(late_z[v])
            if v < last:
                hop_out[1, v] = (far[block(v), :] + dot(got(cor_z, v, split, nb * BLK), eff[1, split:])).astype(BF16)
            else:
                hop_out[1, v] = dot(got(cor_z, v, last * BLK, nb * BLK), eff[1, last * BLK :]).astype(BF16)
            hop(1, v).start()

    stage4(late_x)
    par[split:, :] = gram(got(cor_x, last, split, nb * BLK), eff[0, block(last)])

    @pl.when(has_from)
    def _():
        par[split:, :] += gram(stack(cor_z, 0, last, split, nb * BLK), eff[2, : last * BLK])
        par[block(last), :] += gram(got(cor_z, last, last * BLK, nb * BLK), eff[2, block(last)])

    hop_out[0, last] = par[block(last), :].astype(BF16)
    hop(0, last).start()
    for u in range(nb):
        acc[block(u), :] += dot(got(cor_x, u, 0, (u + 1) * BLK), eff[1, : (u + 1) * BLK])
    for u in range(nb - 1, -1, -1):
        hop(0, nb - 1 - u).wait_recv()
        out_ref[at_block(mine(u)), :] = acc[block(u), :] + hop_in[0, nb - 1 - u].astype(F32)

    @pl.when(has_to)
    def _():
        for v in range(nb):
            hop(1, v).wait_recv()
            out_ref[at_block(mine(v)), :] += hop_in[1, v].astype(F32)

    for c in to_partner:
        c.wait_send()

    @pl.when(has_to)
    def _():
        for c in to_next:
            c.wait_send()

    for group in X + [L]:
        for c in (to_core(group), to_cross(group), share(group)):
            c.wait_send()
    for t in range(nb):
        hop(0, t).wait_send()

    @pl.when(has_from)
    def _():
        for group in Z:
            for c in (to_core(group), to_cross(group), share(group)):
                c.wait_send()
        for t in range(nb):
            hop(1, t).wait_send()


def body(n_genome, n_samp, dosage, effects, depth):
    nb = depth.shape[0]
    samples, variants = dosage.shape
    traits = effects.shape[1]
    half = samples // 2
    dma = pltpu.SemaphoreType.DMA
    pairs = nb * (nb + 1) // 2
    groups_x, groups_z = make_groups(nb)
    n_groups = len(groups_x) + len(groups_z) + 1

    def pair_of(kind, lead, dtype, lead_l=()):
        wide = pltpu.VMEM((nb,) + lead + (HB, variants), dtype)
        return [wide, wide, pltpu.VMEM((pairs,) + lead + (HB, BLK), kind)]

    return pl.pallas_call(
        functools.partial(kernel, n_genome, n_samp, nb, half, 1.0 / (samples * n_samp)),
        out_shape=pltpu.VMEM((variants, traits), F32),
        in_specs=[
            pl.BlockSpec(memory_space=pl.ANY),
            pl.BlockSpec(memory_space=pl.ANY),
            pl.BlockSpec(memory_space=pltpu.SMEM),
        ],
        out_specs=pl.BlockSpec(memory_space=pltpu.VMEM),
        scratch_shapes=[
            pltpu.VMEM((8, BLK), F32),
            pltpu.VMEM((2, 8, BLK), F32),
            pltpu.VMEM((nb, samples, BLK), BF16),
            pltpu.VMEM((nb, half, BLK), BF16),
            pltpu.VMEM((nb, half, BLK), BF16),
            pltpu.VMEM((3, variants, traits), BF16),
            *pair_of(F32, (2,), F32),
            *pair_of(F32, (), F32),
            *pair_of(F32, (), BF16),
            *pair_of(F32, (), BF16),
            *pair_of(BF16, (2,), BF16),
            pltpu.VMEM((variants, traits), F32),
            pltpu.VMEM((variants, traits), F32),
            pltpu.VMEM((variants, traits), F32),
            pltpu.VMEM((2, nb, BLK, traits), BF16),
            pltpu.VMEM((2, nb, BLK, traits), BF16),
            dma((nb,)), dma((nb,)),
            dma((nb + len(PARTS),)), dma((nb + len(PARTS),)),
            dma((nb + len(PARTS),)), dma((nb + len(PARTS),)),
            dma((nb,)), dma((nb,)), dma((nb,)), dma((nb,)), dma((2,)), dma((2,)),
            dma((n_groups,)), dma((n_groups,)), dma((n_groups,)), dma((n_groups,)), dma((n_groups,)), dma((n_groups,)),
            dma((2, nb)), dma((2, nb)),
        ],
        compiler_params=pltpu.CompilerParams(
            collective_id=0, has_side_effects=True, vmem_limit_bytes=60 * 1024 * 1024
        ),
        cost_estimate=pl.CostEstimate(
            flops=2 * 20 * BLK * BLK * samples, bytes_accessed=4 * samples * variants, transcendentals=0
        ),
    )(dosage, effects, depth)


def solution(mesh):
    return jax.shard_map(
        functools.partial(body, mesh.shape["genome"], mesh.shape["samp"]),
        mesh=mesh,
        in_specs=(P("samp", "genome"), P("genome", "samp"), P("genome")),
        out_specs=P("genome", "samp"),
        check_vma=False,
    )
```

```python
import functools

import jax
import jax.numpy as jnp
from jax import lax
from jax.experimental import pallas as pl
from jax.experimental.pallas import tpu as pltpu
from jax.sharding import PartitionSpec as P

BLK = 256
HB = BLK // 2
MESH = pl.DeviceIdType.MESH
F32 = jnp.float32
BF16 = jnp.bfloat16
CONTRACT0 = (((0,), (0,)), ((), ()))
PARTS = (2, 4, 8, 8)


def gram(left, right):
    return lax.dot_general(left, right, CONTRACT0, preferred_element_type=F32)


def dot(left, right):
    return jnp.dot(left, right, preferred_element_type=F32)


def make_groups(nb):
    def cols(t):
        return t * BLK, (t + 1) * BLK

    x = [[(t, nb) + cols(t)] for t in range(1, nb)] + [[(0, nb, 0, HB)]]
    x += [[(u, u + 2, HB, BLK) for u in range(0, nb, 2)]]
    z = [[(0, t) + cols(t)] + ([(t - 1, t) + cols(t - 1)] if t > 1 else []) for t in range(1, nb)]
    z += [[(0, 1, 0, HB)], [(0, 1, HB, BLK)]]
    w = [[(0, 1, 0, HB)], [(0, 1, HB, BLK)]]
    return x, z, w


def kernel(
    n_genome, n_samp, nb, half, scale,
    x_ref, e_ref, depth_ref, out_ref,
    d_ref, dep, own, xbuf, zbuf, eff,
    sum_x, sum_z, sum_w, sum_l, cin_x, cin_z, cin_w, cin_l, yo_x, yo_z, yo_w, yo_l, yi_x, yi_z, yi_w, yi_l,
    cor_x, cor_z, cor_w, cor_l,
    acc, par, far, hop_out, hop_in,
    own_sem, own_e_sem, x_send, x_recv, z_send, z_recv, ex_send, ex_recv, ez_send, ez_recv, ds_send, ds_recv,
    a_send, a_recv, b_send, b_recv, c_send, c_recv, h_send, h_recv,
):
    g = lax.axis_index("genome")
    s = lax.axis_index("samp")
    q = lax.rem(g, 2)
    sign = 1 - 2 * q
    partner = g + sign
    z_from = g + 2 * sign
    z_to = g - 2 * sign
    has_from = jnp.logical_and(z_from >= 0, z_from < n_genome)
    has_to = jnp.logical_and(z_to >= 0, z_to < n_genome)
    last = nb - 1

    def mine(u):
        return u + q * (nb - 1 - 2 * u)

    def other(u):
        return nb - 1 - mine(u)

    core = lax.rem(s, 2)
    core_mate = s + 1 - 2 * core
    cross_mate = lax.rem(s + 2, n_samp)

    def remote(src, dst, ss, rsem, gg, sss):
        return pltpu.make_async_remote_copy(
            src_ref=src, dst_ref=dst, send_sem=ss, recv_sem=rsem,
            device_id=(gg, sss), device_id_type=MESH,
        )

    def at_block(b):
        return pl.ds(pl.multiple_of(b * BLK, BLK), BLK)

    def half_rows(which, low, high):
        return pl.ds(pl.multiple_of(which * half + low, 16), high - low)

    barrier = pltpu.get_barrier_semaphore()
    for mate in (core_mate, cross_mate):
        pl.semaphore_signal(barrier, inc=1, device_id=(g, mate), device_id_type=MESH)
    pl.semaphore_signal(barrier, inc=1, device_id=(partner, s), device_id_type=MESH)

    @pl.when(has_from)
    def _():
        pl.semaphore_signal(barrier, inc=1, device_id=(z_from, s), device_id_type=MESH)

    @pl.when(has_to)
    def _():
        pl.semaphore_signal(barrier, inc=1, device_id=(z_to, s), device_id_type=MESH)

    own_copies = [
        pltpu.make_async_copy(x_ref.at[:, at_block(mine(u))], own.at[u], own_sem.at[u]) for u in range(nb)
    ]
    own_effects = [
        pltpu.make_async_copy(e_ref.at[at_block(mine(u)), :], eff.at[0, u * BLK : (u + 1) * BLK], own_e_sem.at[u])
        for u in range(nb)
    ]
    for c in own_copies + own_effects:
        c.start()
    for u in range(nb):
        d_ref[u : u + 1, :] = jnp.full((1, BLK), depth_ref[mine(u)].astype(F32))
    pl.semaphore_wait(
        barrier, 3 + has_from.astype(jnp.int32) + has_to.astype(jnp.int32)
    )

    pieces = []
    for part in PARTS:
        low = pieces[-1][1] if pieces else 0
        pieces.append((low, low + half // part))

    def x_part(t, low, high, left, right, n):
        src = pl.ds(pl.multiple_of(other(t) * BLK + left, HB), right - left)
        return remote(
            x_ref.at[half_rows(1 - q, low, high), src], xbuf.at[t, low:high, left:right],
            x_send.at[n], x_recv.at[n], partner, s,
        )

    def z_part(v, low, high, left, right, n):
        src = pl.ds(pl.multiple_of(mine(v) * BLK + left, HB), right - left)
        return remote(
            x_ref.at[half_rows(q, low, high), src], zbuf.at[v, low:high, left:right],
            z_send.at[n], z_recv.at[n], z_to, s,
        )

    x_copies = [x_part(k + 1, 0, half, 0, BLK, k) for k in range(last)] + [x_part(0, 0, half, 0, HB, last)]
    z_copies = [z_part(k, 0, half, 0, BLK, k) for k in range(last)] + [z_part(last, 0, half, 0, HB, last)]
    x_last = [x_part(0, low, high, HB, BLK, nb + n) for n, (low, high) in enumerate(pieces)]
    z_last = [z_part(last, low, high, HB, BLK, nb + n) for n, (low, high) in enumerate(pieces)]
    e_x = [
        remote(e_ref.at[at_block(other(t)), :], eff.at[1, t * BLK : (t + 1) * BLK], ex_send.at[t], ex_recv.at[t], partner, s)
        for t in range(nb)
    ]
    e_z = [
        remote(e_ref.at[at_block(mine(v)), :], eff.at[2, v * BLK : (v + 1) * BLK], ez_send.at[v], ez_recv.at[v], z_to, s)
        for v in range(nb)
    ]
    d_x = remote(d_ref, dep.at[0], ds_send.at[0], ds_recv.at[0], partner, s)
    d_z = remote(d_ref, dep.at[1], ds_send.at[1], ds_recv.at[1], z_to, s)
    to_partner = [d_x] + x_copies + x_last + e_x[::-1]
    to_next = [d_z] + z_copies + z_last + e_z
    for c in to_partner:
        c.start()

    @pl.when(has_to)
    def _():
        for c in to_next:
            c.start()

    counter = [0]

    def label(steps, refs):
        out = []
        for step in steps:
            out.append([(counter[0] + n, refs) + gr for n, gr in enumerate(step)])
            counter[0] += len(step)
        return out

    groups_x, groups_z, groups_w = make_groups(nb)
    X = label(groups_x, (sum_x, cin_x, yo_x, yi_x, cor_x))
    Z = label(groups_z, (sum_z, cin_z, yo_z, yi_z, cor_z))
    W = label(groups_w, (sum_w, cin_w, yo_w, yi_w, cor_w))
    L = label([[(0, nb * (nb + 1) // 2, 0, BLK)]], (sum_l, cin_l, yo_l, yi_l, cor_l))[0][0]

    def to_core(group):
        i, (total, cin, _, _, _), low, high, left, right = group
        return remote(
            total.at[low:high, 1 - core, :, left:right], cin.at[low:high, :, left:right],
            a_send.at[i], a_recv.at[i], g, core_mate,
        )

    def to_cross(group):
        i, (_, _, y_out, y_in, _), low, high, left, right = group
        return remote(
            y_out.at[low:high, :, left:right], y_in.at[low:high, :, left:right],
            b_send.at[i], b_recv.at[i], g, cross_mate,
        )

    def share(group):
        i, (_, _, _, _, corr), low, high, left, right = group
        part = corr.at[low:high, core, :, left:right]
        return remote(part, part, c_send.at[i], c_recv.at[i], g, core_mate)

    def stage1(group):
        to_core(group).start()

    def stage2(group):
        i, (total, cin, y_out, _, _), low, high, left, right = group
        to_core(group).wait_recv()
        for a in range(low, high):
            value = total[a, core, :, left:right] + cin[a, :, left:right]
            total[a, core, :, left:right] = value
            y_out[a, :, left:right] = value.astype(y_out.dtype)
        to_cross(group).start()

    def stage3(group):
        i, (total, _, _, y_in, corr), low, high, left, right = group
        to_cross(group).wait_recv()
        for a in range(low, high):
            value = total[a, core, :, left:right] + y_in[a, :, left:right].astype(F32)
            corr[a, core, :, left:right] = value.astype(BF16)
        share(group).start()

    def stage4(group):
        share(group).wait_recv()

    def weight(drow, k, width):
        return jnp.where(drow >= jnp.asarray(k, F32), F32(scale), F32(0.0))[:, :width]

    def row_of(ref, n):
        return ref[pl.ds(n, 1), :]

    def x_weight(t, u, width):
        drow = jnp.where(q == 0, row_of(d_ref, u), row_of(dep.at[0], nb - 1 - t))
        return weight(drow, (nb + t - u), width)

    def z_weight(t, v, width):
        drow = jnp.where(q == 0, row_of(dep.at[0], nb - 1 - t), row_of(dep.at[1], v))
        return weight(drow, (nb + v - t), width)

    def put(ref, a, left, right, value):
        for h in range(2):
            ref[a, h, :, left:right] = value[h * HB : (h + 1) * HB]

    def got(ref, a, left, right):
        return ref[a, :, :, left:right].reshape(BLK, right - left)

    def stack(ref, low, high, left, right):
        return ref[low:high, :, :, left:right].reshape((high - low) * BLK, right - left)

    def block(n):
        return slice(n * BLK, (n + 1) * BLK)

    for c in own_copies + own_effects:
        c.wait()

    def local_row(i, carry):
        def local_pair(j, carry):
            full = gram(own[i, :half], own[j, :half]) + gram(own[i, half:], own[j, half:])
            drow = jnp.where(q == 0, row_of(d_ref, i), row_of(d_ref, j))
            full = full * weight(drow, (j - i).astype(F32), BLK)
            put(sum_l, i * (2 * nb - i + 1) // 2 + (j - i), 0, BLK, full)
            return carry

        return lax.fori_loop(i, nb, local_pair, carry)

    lax.fori_loop(0, nb, local_row, 0)
    stage1(L)
    acc[...] = jnp.zeros_like(acc)
    stage2(L)
    d_x.wait_recv()

    @pl.when(has_from)
    def _():
        d_z.wait_recv()

    def x_grams(t, left, right):
        def pair(u, carry):
            full = gram(own[u, half_rows(q, 0, half), :], xbuf[t, :, left:right])
            put(sum_x, u, t * BLK + left, t * BLK + right, full * x_weight(t, u, right - left))
            return carry

        lax.fori_loop(t, nb, pair, 0)

    def z_grams(low, high, t, left, right):
        def pair(v, carry):
            full = gram(zbuf[v], xbuf[t, :, left:right])
            put(sum_z, v, t * BLK + left, t * BLK + right, full * z_weight(t, v, right - left))
            return carry

        lax.fori_loop(low, high, pair, 0)

    def local_products():
        def local_row(i, carry):
            def local_pair(j, carry):
                corr = got(cor_l, i * (2 * nb - i + 1) // 2 + (j - i), 0, BLK)
                acc[at_block(i), :] += dot(corr, eff[0, at_block(j), :])

                @pl.when(j > i)
                def _():
                    acc[at_block(j), :] += gram(corr, eff[0, at_block(i), :])

                return carry

            return lax.fori_loop(i, nb, local_pair, carry)

        lax.fori_loop(0, nb, local_row, 0)

    def from_groups(k):
        return Z[k] + (W[k - last] if k >= last else [])

    def both(stage, k):
        for group in X[k]:
            stage(group)

        @pl.when(has_from)
        def _():
            for group in from_groups(k):
                stage(group)

    for k in range(nb):
        t, left, right = (k + 1, 0, BLK) if k < last else (0, 0, HB)
        x_copies[k].wait_recv()
        x_grams(t, left, right)
        stage1(X[k][0])

        @pl.when(has_from)
        def _():
            z_copies[k].wait_recv()
            if k < last:
                z_grams(0, t, t, left, right)
                if k:
                    z_grams(k, k + 1, k, left, right)
            else:
                z_grams(0, 1, 0, left, right)
                full = gram(xbuf[last], zbuf[last, :, left:right])
                put(sum_w, 0, left, right, full * z_weight(last, last, HB))
            for group in from_groups(k):
                stage1(group)

        both(stage2, k)
        if k == 1:
            stage3(L)
            both(stage3, 0)
            stage4(L)
            local_products()
            both(stage4, 0)
        if k == 2:
            both(stage3, 1)
            both(stage4, 1)

    late_z, late_w = Z[nb][0], W[1][0]
    for n, (low, high) in enumerate(pieces):
        final = n == len(pieces) - 1

        def add(ref, a, value, factor):
            for h in range(2):
                part = value[h * HB : (h + 1) * HB]
                if n:
                    part = ref[a, h, :, HB:BLK] + part
                ref[a, h, :, HB:BLK] = part * factor if final else part

        if n == 1:
            both(stage3, 2)
        x_last[n].wait_recv()

        @pl.when(has_from)
        def _():
            full = gram(zbuf[0, low:high], xbuf[0, low:high, HB:])
            add(sum_z, 0, full, z_weight(0, 0, HB) if final else None)
            if final:
                stage1(late_z)
            z_last[n].wait_recv()
            full = gram(xbuf[last, low:high], zbuf[last, low:high, HB:])
            add(sum_w, 0, full, z_weight(last, last, HB) if final else None)
            if final:
                stage1(late_w)

        for u in range(nb):
            full = gram(own[u, half_rows(q, low, high), :], xbuf[0, low:high, HB:])
            add(sum_x, u, full, x_weight(0, u, HB) if final else None)
            if final and u % 2:
                stage1(X[nb][u // 2])

    @pl.when(has_from)
    def _():
        stage2(late_z)
        stage2(late_w)

    for group in X[nb]:
        stage2(group)
    both(stage4, 2)
    both(stage3, last)

    def hop(n, t, low=0, high=BLK):
        i = nb if low else t
        return remote(
            hop_out.at[n, t, low:high], hop_in.at[n, t, low:high], h_send.at[n, i], h_recv.at[n, i],
            partner if n == 0 else z_from, s,
        )

    hops_x = [hop(0, t) for t in range(1, nb)] + [hop(0, 0, 0, HB), hop(0, 0, HB, BLK)]
    hops_z = [hop(1, v) for v in range(nb)]

    for t in range(1, nb):
        par[block(t), :] = gram(stack(cor_x, t, nb, t * BLK, (t + 1) * BLK), eff[0, t * BLK :])
    both(stage4, last)
    par[:HB, :] = gram(stack(cor_x, 0, nb, 0, HB), eff[0])

    @pl.when(has_from)
    def _():
        e_z[0].wait_recv()
        par[:HB, :] += gram(got(cor_z, 0, 0, HB), eff[2, block(0)])

    for t in range(1, last):
        @pl.when(has_from)
        def _():
            e_z[t].wait_recv()
            par[block(t), :] += gram(stack(cor_z, 0, t + 1, t * BLK, (t + 1) * BLK), eff[2, : (t + 1) * BLK])

        hop_out[0, t] = par[block(t), :].astype(BF16)
        hops_x[t - 1].start()

    hop_out[0, 0, :HB] = par[:HB, :].astype(BF16)
    hops_x[nb - 1].start()
    e_x[last].wait_recv()
    for v in range(last - 1, 0, -1):
        e_x[v].wait_recv()

        @pl.when(has_from)
        def _():
            hop_out[1, v] = dot(got(cor_z, v, v * BLK, nb * BLK), eff[1, v * BLK :]).astype(BF16)
            hops_z[v].start()

    @pl.when(has_from)
    def _():
        e_z[last].wait_recv()
        par[block(last), :] += gram(stack(cor_z, 0, last, last * BLK, nb * BLK), eff[2, : last * BLK])
        far[block(0), :] = dot(got(cor_z, 0, BLK, nb * BLK), eff[1, BLK:])
        stage3(late_z)
        stage3(late_w)

    e_x[0].wait_recv()

    @pl.when(has_from)
    def _():
        stage4(late_z)
        hop_out[1, 0] = (far[block(0), :] + dot(got(cor_z, 0, 0, BLK), eff[1, block(0)])).astype(BF16)
        hops_z[0].start()
        stage4(late_w)
        corr = got(cor_w, 0, 0, BLK)
        hop_out[1, last] = gram(corr, eff[1, block(last)]).astype(BF16)
        hops_z[last].start()
        par[block(last), :] += dot(corr, eff[2, block(last)])

    hop_out[0, last] = par[block(last), :].astype(BF16)
    hops_x[last - 1].start()
    for group in X[nb]:
        stage3(group)
    for group in X[nb]:
        stage4(group)
    par[HB:BLK, :] = gram(stack(cor_x, 0, nb, HB, BLK), eff[0])

    @pl.when(has_from)
    def _():
        par[HB:BLK, :] += gram(got(cor_z, 0, HB, BLK), eff[2, block(0)])

    hop_out[0, 0, HB:] = par[HB:BLK, :].astype(BF16)
    hops_x[nb].start()
    for u in range(nb):
        out_ref[at_block(mine(u)), :] = acc[block(u), :] + dot(got(cor_x, u, 0, (u + 1) * BLK), eff[1, : (u + 1) * BLK])
    for t in range(1, nb):
        hops_x[t - 1].wait_recv()
        out_ref[at_block(other(t)), :] += hop_in[0, t].astype(F32)

    @pl.when(has_to)
    def _():
        for v in list(range(last - 1, -1, -1)) + [last]:
            hops_z[v].wait_recv()
            out_ref[at_block(mine(v)), :] += hop_in[1, v].astype(F32)

    hops_x[nb - 1].wait_recv()
    hops_x[nb].wait_recv()
    out_ref[at_block(other(0)), :] += hop_in[0, 0].astype(F32)

    for c in to_partner:
        c.wait_send()

    @pl.when(has_to)
    def _():
        for c in to_next:
            c.wait_send()

    for group in sum(X, [L]):
        for c in (to_core(group), to_cross(group), share(group)):
            c.wait_send()
    for c in hops_x:
        c.wait_send()

    @pl.when(has_from)
    def _():
        for group in sum(Z + W, []):
            for c in (to_core(group), to_cross(group), share(group)):
                c.wait_send()
        for c in hops_z:
            c.wait_send()


def body(n_genome, n_samp, dosage, effects, depth):
    nb = depth.shape[0]
    samples, variants = dosage.shape
    traits = effects.shape[1]
    half = samples // 2
    dma = pltpu.SemaphoreType.DMA
    pairs = nb * (nb + 1) // 2
    n_groups = 1 + sum(len(step) for steps in make_groups(nb) for step in steps)

    def pair_of(kind, lead, dtype):
        wide = pltpu.VMEM((nb,) + lead + (HB, variants), dtype)
        return [
            wide, wide, pltpu.VMEM((1,) + lead + (HB, BLK), dtype), pltpu.VMEM((pairs,) + lead + (HB, BLK), kind),
        ]

    return pl.pallas_call(
        functools.partial(kernel, n_genome, n_samp, nb, half, 1.0 / (samples * n_samp)),
        out_shape=pltpu.VMEM((variants, traits), F32),
        in_specs=[
            pl.BlockSpec(memory_space=pl.ANY),
            pl.BlockSpec(memory_space=pl.ANY),
            pl.BlockSpec(memory_space=pltpu.SMEM),
        ],
        out_specs=pl.BlockSpec(memory_space=pltpu.VMEM),
        scratch_shapes=[
            pltpu.VMEM((8, BLK), F32),
            pltpu.VMEM((2, 8, BLK), F32),
            pltpu.VMEM((nb, samples, BLK), BF16),
            pltpu.VMEM((nb, half, BLK), BF16),
            pltpu.VMEM((nb, half, BLK), BF16),
            pltpu.VMEM((3, variants, traits), BF16),
            *pair_of(F32, (2,), F32),
            *pair_of(F32, (), F32),
            *pair_of(F32, (), BF16),
            *pair_of(F32, (), BF16),
            *pair_of(BF16, (2,), BF16),
            pltpu.VMEM((variants, traits), F32),
            pltpu.VMEM((variants, traits), F32),
            pltpu.VMEM((variants, traits), F32),
            pltpu.VMEM((2, nb, BLK, traits), BF16),
            pltpu.VMEM((2, nb, BLK, traits), BF16),
            dma((nb,)), dma((nb,)),
            dma((nb + len(PARTS),)), dma((nb + len(PARTS),)),
            dma((nb + len(PARTS),)), dma((nb + len(PARTS),)),
            dma((nb,)), dma((nb,)), dma((nb,)), dma((nb,)), dma((2,)), dma((2,)),
            dma((n_groups,)), dma((n_groups,)), dma((n_groups,)), dma((n_groups,)), dma((n_groups,)), dma((n_groups,)),
            dma((2, nb + 1)), dma((2, nb + 1)),
        ],
        compiler_params=pltpu.CompilerParams(
            collective_id=0, has_side_effects=True, vmem_limit_bytes=60 * 1024 * 1024
        ),
        cost_estimate=pl.CostEstimate(
            flops=2 * 20 * BLK * BLK * samples, bytes_accessed=4 * samples * variants, transcendentals=0
        ),
    )(dosage, effects, depth)


def solution(mesh):
    return jax.shard_map(
        functools.partial(body, mesh.shape["genome"], mesh.shape["samp"]),
        mesh=mesh,
        in_specs=(P("samp", "genome"), P("genome", "samp"), P("genome")),
        out_specs=P("genome", "samp"),
        check_vma=False,
    )
```

```python
import functools

import jax
import jax.numpy as jnp
from jax import lax
from jax.experimental import pallas as pl
from jax.experimental.pallas import tpu as pltpu
from jax.sharding import PartitionSpec as P

BLK = 256
HB = BLK // 2
MESH = pl.DeviceIdType.MESH
F32 = jnp.float32
BF16 = jnp.bfloat16
CONTRACT0 = (((0,), (0,)), ((), ()))
PARTS = (2, 4, 8, 8)


def gram(left, right):
    return lax.dot_general(left, right, CONTRACT0, preferred_element_type=F32)


def dot(left, right):
    return jnp.dot(left, right, preferred_element_type=F32)


def make_groups(nb):
    def cols(t):
        return t * BLK, (t + 1) * BLK

    x = [[(t, nb) + cols(t)] for t in range(1, nb)] + [[(0, nb, 0, HB)]]
    z = [[(0, t) + cols(t)] + ([(t - 1, t) + cols(t - 1)] if t > 1 else []) for t in range(1, nb)]
    z += [[(0, 1, 0, HB)]]
    spots = [0, nb * BLK // 2, nb * BLK, (nb + 1) * BLK, (nb + 2) * BLK, (nb + 3) * BLK]
    late = [[(0, 1) + spot] for spot in zip(spots[:-1], spots[1:])]
    return x, z, late


def kernel(
    n_genome, n_samp, nb, half, scale,
    x_ref, e_ref, depth_ref, out_ref,
    d_ref, dep, own, xbuf, zbuf, eff,
    sum_x, sum_z, sum_t, sum_l, cin_x, cin_z, cin_t, cin_l, yo_x, yo_z, yo_t, yo_l, yi_x, yi_z, yi_t, yi_l,
    cor_x, cor_z, cor_t, cor_l,
    acc, par, far, hop_out, hop_in, pair_e, mate_far, last_sum, last_out, last_in,
    own_sem, own_e_sem, x_send, x_recv, z_send, z_recv, ex_send, ex_recv, ez_send, ez_recv, ds_send, ds_recv,
    a_send, a_recv, b_send, b_recv, c_send, c_recv, h_send, h_recv, m_send, m_recv, l_send, l_recv,
):
    g = lax.axis_index("genome")
    s = lax.axis_index("samp")
    q = lax.rem(g, 2)
    sign = 1 - 2 * q
    partner = g + sign
    z_from = g + 2 * sign
    z_to = g - 2 * sign
    has_from = jnp.logical_and(z_from >= 0, z_from < n_genome)
    has_to = jnp.logical_and(z_to >= 0, z_to < n_genome)
    last = nb - 1

    def mine(u):
        return u + q * (nb - 1 - 2 * u)

    def other(u):
        return nb - 1 - mine(u)

    core = lax.rem(s, 2)
    core_mate = s + 1 - 2 * core
    cross_mate = lax.rem(s + 2, n_samp)

    def remote(src, dst, ss, rsem, gg, sss):
        return pltpu.make_async_remote_copy(
            src_ref=src, dst_ref=dst, send_sem=ss, recv_sem=rsem,
            device_id=(gg, sss), device_id_type=MESH,
        )

    def at_block(b):
        return pl.ds(pl.multiple_of(b * BLK, BLK), BLK)

    def half_rows(which, low, high):
        return pl.ds(pl.multiple_of(which * half + low, 16), high - low)

    barrier = pltpu.get_barrier_semaphore()
    for mate in (core_mate, cross_mate):
        pl.semaphore_signal(barrier, inc=1, device_id=(g, mate), device_id_type=MESH)
    for mate in (s, core_mate):
        pl.semaphore_signal(barrier, inc=1, device_id=(partner, mate), device_id_type=MESH)

    @pl.when(has_from)
    def _():
        pl.semaphore_signal(barrier, inc=1, device_id=(z_from, s), device_id_type=MESH)

    @pl.when(has_to)
    def _():
        pl.semaphore_signal(barrier, inc=1, device_id=(z_to, s), device_id_type=MESH)

    own_copies = [
        pltpu.make_async_copy(x_ref.at[:, at_block(mine(u))], own.at[u], own_sem.at[u]) for u in range(nb)
    ]
    own_effects = [
        pltpu.make_async_copy(e_ref.at[at_block(mine(u)), :], eff.at[0, u * BLK : (u + 1) * BLK], own_e_sem.at[u])
        for u in range(nb)
    ]
    for c in own_copies + own_effects:
        c.start()
    for u in range(nb):
        d_ref[u : u + 1, :] = jnp.full((1, BLK), depth_ref[mine(u)].astype(F32))
    pl.semaphore_wait(
        barrier, 4 + has_from.astype(jnp.int32) + has_to.astype(jnp.int32)
    )

    pieces = []
    for part in PARTS:
        low = pieces[-1][1] if pieces else 0
        pieces.append((low, low + half // part))

    def x_part(t, low, high, left, right, n):
        src = pl.ds(pl.multiple_of(other(t) * BLK + left, HB), right - left)
        return remote(
            x_ref.at[half_rows(1 - q, low, high), src], xbuf.at[t, low:high, left:right],
            x_send.at[n], x_recv.at[n], partner, s,
        )

    def z_part(v, low, high, left, right, n):
        src = pl.ds(pl.multiple_of(mine(v) * BLK + left, HB), right - left)
        return remote(
            x_ref.at[half_rows(q, low, high), src], zbuf.at[v, low:high, left:right],
            z_send.at[n], z_recv.at[n], z_to, s,
        )

    x_copies = [x_part(k + 1, 0, half, 0, BLK, k) for k in range(last)] + [x_part(0, 0, half, 0, HB, last)]
    z_copies = [z_part(k, 0, half, 0, BLK, k) for k in range(last)] + [z_part(last, 0, half, 0, HB, last)]
    x_last = [x_part(0, low, high, HB, BLK, nb + n) for n, (low, high) in enumerate(pieces)]
    z_last = [z_part(last, low, high, HB, BLK, nb + n) for n, (low, high) in enumerate(pieces)]
    e_x = [
        remote(e_ref.at[at_block(other(t)), :], eff.at[1, t * BLK : (t + 1) * BLK], ex_send.at[t], ex_recv.at[t], partner, s)
        for t in range(nb)
    ]
    e_z = [
        remote(e_ref.at[at_block(mine(v)), :], eff.at[2, v * BLK : (v + 1) * BLK], ez_send.at[v], ez_recv.at[v], z_to, s)
        for v in range(nb)
    ]
    d_x = remote(d_ref, dep.at[0], ds_send.at[0], ds_recv.at[0], partner, s)
    d_z = remote(d_ref, dep.at[1], ds_send.at[1], ds_recv.at[1], z_to, s)
    e_mate = [
        remote(e_ref.at[at_block(mine(u)), :], pair_e.at[u * BLK : (u + 1) * BLK], m_send.at[u], m_recv.at[u], g, core_mate)
        for u in range(nb)
    ]
    f_mate = remote(eff.at[2, :BLK], mate_far, m_send.at[nb], m_recv.at[nb], g, core_mate)
    to_partner = [d_x] + x_copies + x_last + e_x[::-1]
    to_next = [d_z] + z_copies + z_last + e_z
    for c in to_partner + e_mate:
        c.start()

    @pl.when(has_to)
    def _():
        for c in to_next:
            c.start()

    counter = [0]

    def label(steps, refs):
        out = []
        for step in steps:
            out.append([(counter[0] + n, refs) + gr for n, gr in enumerate(step)])
            counter[0] += len(step)
        return out

    groups_x, groups_z, groups_t = make_groups(nb)
    X = label(groups_x, (sum_x, cin_x, yo_x, yi_x, cor_x))
    Z = label(groups_z, (sum_z, cin_z, yo_z, yi_z, cor_z))
    T = label(groups_t, (sum_t, cin_t, yo_t, yi_t, cor_t))
    late_x, (late_z, late_w, early_w) = [T[0][0], T[1][0]], [step[0] for step in T[2:]]
    SPOT_Z, SPOT_W, SPOT_V = nb * BLK, (nb + 1) * BLK, (nb + 2) * BLK
    L = label([[(0, nb * (nb + 1) // 2, 0, BLK)]], (sum_l, cin_l, yo_l, yi_l, cor_l))[0][0]

    def to_core(group):
        i, (total, cin, _, _, _), low, high, left, right = group
        return remote(
            total.at[low:high, 1 - core, :, left:right], cin.at[low:high, :, left:right],
            a_send.at[i], a_recv.at[i], g, core_mate,
        )

    def to_cross(group):
        i, (_, _, y_out, y_in, _), low, high, left, right = group
        return remote(
            y_out.at[low:high, :, left:right], y_in.at[low:high, :, left:right],
            b_send.at[i], b_recv.at[i], g, cross_mate,
        )

    def share(group):
        i, (_, _, _, _, corr), low, high, left, right = group
        part = corr.at[low:high, core, :, left:right]
        return remote(part, part, c_send.at[i], c_recv.at[i], g, core_mate)

    def stage1(group):
        to_core(group).start()

    def stage2(group):
        i, (total, cin, y_out, _, _), low, high, left, right = group
        to_core(group).wait_recv()
        for a in range(low, high):
            value = total[a, core, :, left:right] + cin[a, :, left:right]
            total[a, core, :, left:right] = value
            y_out[a, :, left:right] = value.astype(y_out.dtype)
        to_cross(group).start()

    def stage3(group):
        i, (total, _, _, y_in, corr), low, high, left, right = group
        to_cross(group).wait_recv()
        for a in range(low, high):
            value = total[a, core, :, left:right] + y_in[a, :, left:right].astype(F32)
            corr[a, core, :, left:right] = value.astype(BF16)
        share(group).start()

    def stage4(group):
        share(group).wait_recv()

    def weight(drow, k, width):
        return jnp.where(drow >= jnp.asarray(k, F32), F32(scale), F32(0.0))[:, :width]

    def row_of(ref, n):
        return ref[pl.ds(n, 1), :]

    def x_weight(t, u, width):
        drow = jnp.where(q == 0, row_of(d_ref, u), row_of(dep.at[0], nb - 1 - t))
        return weight(drow, (nb + t - u), width)

    def z_weight(t, v, width):
        drow = jnp.where(q == 0, row_of(dep.at[0], nb - 1 - t), row_of(dep.at[1], v))
        return weight(drow, (nb + v - t), width)

    def put(ref, a, left, right, value):
        for h in range(2):
            ref[a, h, :, left:right] = value[h * HB : (h + 1) * HB]

    def got(ref, a, left, right):
        return ref[a, :, :, left:right].reshape(BLK, right - left)

    def stack(ref, low, high, left, right):
        return ref[low:high, :, :, left:right].reshape((high - low) * BLK, right - left)

    def block(n):
        return slice(n * BLK, (n + 1) * BLK)

    for c in own_copies + own_effects:
        c.wait()

    def local_row(i, carry):
        def local_pair(j, carry):
            full = gram(own[i, :half], own[j, :half]) + gram(own[i, half:], own[j, half:])
            drow = jnp.where(q == 0, row_of(d_ref, i), row_of(d_ref, j))
            full = full * weight(drow, (j - i).astype(F32), BLK)
            put(sum_l, i * (2 * nb - i + 1) // 2 + (j - i), 0, BLK, full)
            return carry

        return lax.fori_loop(i, nb, local_pair, carry)

    lax.fori_loop(0, nb, local_row, 0)
    stage1(L)
    acc[...] = jnp.zeros_like(acc)
    stage2(L)
    d_x.wait_recv()

    @pl.when(has_from)
    def _():
        d_z.wait_recv()

    def x_grams(t, left, right):
        def pair(u, carry):
            full = gram(own[u, half_rows(q, 0, half), :], xbuf[t, :, left:right])
            put(sum_x, u, t * BLK + left, t * BLK + right, full * x_weight(t, u, right - left))
            return carry

        lax.fori_loop(t, nb, pair, 0)

    def z_grams(low, high, t, left, right):
        def pair(v, carry):
            full = gram(zbuf[v], xbuf[t, :, left:right])
            put(sum_z, v, t * BLK + left, t * BLK + right, full * z_weight(t, v, right - left))
            return carry

        lax.fori_loop(low, high, pair, 0)

    def local_products():
        def local_row(i, carry):
            def local_pair(j, carry):
                corr = got(cor_l, i * (2 * nb - i + 1) // 2 + (j - i), 0, BLK)
                acc[at_block(i), :] += dot(corr, eff[0, at_block(j), :])

                @pl.when(j > i)
                def _():
                    acc[at_block(j), :] += gram(corr, eff[0, at_block(i), :])

                return carry

            return lax.fori_loop(i, nb, local_pair, carry)

        lax.fori_loop(0, nb, local_row, 0)

    def from_groups(k):
        return Z[k] + ([early_w] if k == last else [])

    def both(stage, k):
        for group in X[k]:
            stage(group)

        @pl.when(has_from)
        def _():
            for group in from_groups(k):
                stage(group)

    for k in range(nb):
        t, left, right = (k + 1, 0, BLK) if k < last else (0, 0, HB)
        x_copies[k].wait_recv()
        x_grams(t, left, right)
        stage1(X[k][0])

        @pl.when(has_from)
        def _():
            z_copies[k].wait_recv()
            if k < last:
                z_grams(0, t, t, left, right)
                if k:
                    z_grams(k, k + 1, k, left, right)
            else:
                z_grams(0, 1, 0, left, right)
                full = gram(zbuf[last, :, left:right], xbuf[last]) * z_weight(last, last, BLK)
                for h in range(2):
                    sum_t[0, h, :, SPOT_V : SPOT_V + BLK] = full[h * HB // 2 : (h + 1) * HB // 2]
            for group in from_groups(k):
                stage1(group)

        both(stage2, k)
        if k == 1:
            stage3(L)
            both(stage3, 0)
            stage4(L)
            local_products()
            both(stage4, 0)
        if k == 2:
            both(stage3, 1)
            both(stage4, 1)

    for n, (low, high) in enumerate(pieces):
        final = n == len(pieces) - 1

        def add(left, value, factor):
            for h in range(2):
                part = value[h * HB // 2 : (h + 1) * HB // 2]
                if n:
                    part = sum_t[0, h, :, left : left + BLK] + part
                sum_t[0, h, :, left : left + BLK] = part * factor if final else part

        if n == 1:
            both(stage3, 2)
        x_last[n].wait_recv()
        piece = xbuf[0, low:high, HB:].T

        @pl.when(has_from)
        def _():
            add(SPOT_Z, dot(piece, zbuf[0, low:high]), z_weight(0, 0, BLK) if final else None)
            if final:
                stage1(late_z)
            z_last[n].wait_recv()
            full = dot(zbuf[last, low:high, HB:].T, xbuf[last, low:high])
            add(SPOT_W, full, z_weight(last, last, BLK) if final else None)
            if final:
                stage1(late_w)

        for u in range(nb):
            full = dot(piece, own[u, half_rows(q, low, high), :])
            add(u * BLK, full, x_weight(0, u, BLK) if final else None)
            if final and u % (nb // 2) == nb // 2 - 1:
                stage1(late_x[u // (nb // 2)])

    @pl.when(has_from)
    def _():
        stage2(late_z)
        stage2(late_w)

    for group in late_x:
        stage2(group)
    both(stage4, 2)
    both(stage3, last)

    def hop(n, t, low=0, high=BLK):
        i = nb if low else t
        return remote(
            hop_out.at[n, t, low:high], hop_in.at[n, t, low:high], h_send.at[n, i], h_recv.at[n, i],
            partner if n == 0 else z_from, s,
        )

    hops_x = [hop(0, t) for t in range(1, nb)] + [hop(0, 0, 0, HB)]
    hops_last = [
        remote(last_out.at[n], last_in.at[core], l_send.at[n], l_recv.at[core], partner, to)
        for n, to in enumerate((s, core_mate))
    ]
    last_arrivals = [
        remote(last_out.at[0], last_in.at[n], l_send.at[0], l_recv.at[n], partner, s) for n in range(2)
    ]
    hops_z = [hop(1, v) for v in range(last)] + [hop(1, last, 0, HB), hop(1, last, HB, BLK)]

    def late(left, right):
        return cor_t[0, :, :, left:right].reshape(HB, right - left)

    for t in range(1, nb):
        par[block(t), :] = gram(stack(cor_x, t, nb, t * BLK, (t + 1) * BLK), eff[0, t * BLK :])
    both(stage4, last)
    par[:HB, :] = gram(stack(cor_x, 0, nb, 0, HB), eff[0])

    @pl.when(has_from)
    def _():
        e_z[0].wait_recv()
        f_mate.start()
        par[:HB, :] += gram(got(cor_z, 0, 0, HB), eff[2, block(0)])

    for t in range(1, last):
        @pl.when(has_from)
        def _():
            e_z[t].wait_recv()
            par[block(t), :] += gram(stack(cor_z, 0, t + 1, t * BLK, (t + 1) * BLK), eff[2, : (t + 1) * BLK])

        hop_out[0, t] = par[block(t), :].astype(BF16)
        hops_x[t - 1].start()

    hop_out[0, 0, :HB] = par[:HB, :].astype(BF16)
    hops_x[nb - 1].start()
    e_x[last].wait_recv()

    @pl.when(has_from)
    def _():
        hop_out[1, last, :HB] = dot(late(SPOT_V, SPOT_V + BLK), eff[1, block(last)]).astype(BF16)
        hops_z[last].start()

    for v in range(last - 1, 0, -1):
        e_x[v].wait_recv()

        @pl.when(has_from)
        def _():
            hop_out[1, v] = dot(got(cor_z, v, v * BLK, nb * BLK), eff[1, v * BLK :]).astype(BF16)
            hops_z[v].start()

    @pl.when(has_from)
    def _():
        par[block(last), :] += gram(stack(cor_z, 0, last, last * BLK, nb * BLK), eff[2, : last * BLK])
        far[block(0), :] = dot(got(cor_z, 0, BLK, nb * BLK), eff[1, BLK:])

    @pl.when(has_from)
    def _():
        stage3(late_z)
        stage3(late_w)

    e_x[0].wait_recv()

    @pl.when(has_from)
    def _():
        e_z[last].wait_recv()
        far[block(0), :] += dot(got(cor_z, 0, 0, HB), eff[1, :HB])
        par[block(last), :] += gram(late(SPOT_V, SPOT_V + BLK), eff[2, last * BLK : last * BLK + HB])
        stage4(late_z)
        hop_out[1, 0] = (far[block(0), :] + gram(late(SPOT_Z, SPOT_Z + BLK), eff[1, HB:BLK])).astype(BF16)
        hops_z[0].start()
        stage4(late_w)
        corr = late(SPOT_W, SPOT_W + BLK)
        par[block(last), :] += gram(corr, eff[2, last * BLK + HB :])
        hop_out[1, last, HB:] = dot(corr, eff[1, block(last)]).astype(BF16)
        hops_z[nb].start()

    hop_out[0, last] = par[block(last), :].astype(BF16)
    hops_x[last - 1].start()
    for c in e_mate:
        c.wait_recv()

    def last_rows(left, right):
        return cor_t[0, core, :, left:right]

    @pl.when(has_from)
    def _():
        f_mate.wait_recv()
        rows = last_rows(SPOT_Z, SPOT_Z + BLK)
        last_sum[0] = dot(rows, eff[2, :BLK])
        last_sum[1] = dot(rows, mate_far[...])

    @pl.when(jnp.logical_not(has_from))
    def _():
        last_sum[...] = jnp.zeros_like(last_sum)

    middle = nb * BLK // 2
    stage3(late_x[0])
    last_sum[0] += dot(last_rows(0, middle), eff[0, :middle])
    last_sum[1] += dot(last_rows(0, middle), pair_e[:middle])
    stage3(late_x[1])
    for n, effects in enumerate((eff.at[0], pair_e)):
        value = last_sum[n] + dot(last_rows(middle, nb * BLK), effects[middle:])
        last_out[n] = value.astype(BF16)
        hops_last[n].start()

    for group in late_x:
        stage4(group)
    acc[...] += gram(late(0, nb * BLK), eff[1, HB:BLK])
    for u in range(nb):
        early = acc[block(u), :] + dot(got(cor_x, u, 0, HB), eff[1, :HB])
        if u:
            early += dot(got(cor_x, u, BLK, (u + 1) * BLK), eff[1, BLK : (u + 1) * BLK])
        out_ref[at_block(mine(u)), :] = early
    for c in to_partner + e_mate:
        c.wait_send()

    @pl.when(has_to)
    def _():
        for c in to_next:
            c.wait_send()

    for group in sum(X, [L]) + late_x:
        for c in (to_core(group), to_cross(group), share(group)):
            c.wait_send()

    @pl.when(has_from)
    def _():
        f_mate.wait_send()
        for group in sum(Z, [late_z, late_w, early_w]):
            for c in (to_core(group), to_cross(group), share(group)):
                c.wait_send()

    for t in range(1, nb):
        hops_x[t - 1].wait_recv()
        out_ref[at_block(other(t)), :] += hop_in[0, t].astype(F32)

    @pl.when(has_to)
    def _():
        for v in list(range(last - 1, -1, -1)) + [last]:
            hops_z[v].wait_recv()
            if v == last:
                hops_z[nb].wait_recv()
            out_ref[at_block(mine(v)), :] += hop_in[1, v].astype(F32)

    hops_x[nb - 1].wait_recv()
    first = pl.ds(pl.multiple_of(other(0) * BLK, BLK), HB)
    out_ref[first, :] += hop_in[0, 0, :HB].astype(F32)
    for n, c in enumerate(last_arrivals):
        c.wait_recv()
        rows = pl.ds(pl.multiple_of(other(0) * BLK + HB + n * (HB // 2), HB // 2), HB // 2)
        out_ref[rows, :] += last_in[n].astype(F32)
    for c in hops_x + hops_last:
        c.wait_send()

    @pl.when(has_from)
    def _():
        for c in hops_z:
            c.wait_send()


def body(n_genome, n_samp, dosage, effects, depth):
    nb = depth.shape[0]
    samples, variants = dosage.shape
    traits = effects.shape[1]
    half = samples // 2
    dma = pltpu.SemaphoreType.DMA
    pairs = nb * (nb + 1) // 2
    n_groups = 1 + sum(len(step) for steps in make_groups(nb) for step in steps)

    def pair_of(kind, lead, dtype):
        wide = pltpu.VMEM((nb,) + lead + (HB, variants), dtype)
        return [
            wide, wide, pltpu.VMEM((1,) + lead + (HB // 2, (nb + 3) * BLK), dtype), pltpu.VMEM((pairs,) + lead + (HB, BLK), kind),
        ]

    return pl.pallas_call(
        functools.partial(kernel, n_genome, n_samp, nb, half, 1.0 / (samples * n_samp)),
        out_shape=pltpu.VMEM((variants, traits), F32),
        in_specs=[
            pl.BlockSpec(memory_space=pl.ANY),
            pl.BlockSpec(memory_space=pl.ANY),
            pl.BlockSpec(memory_space=pltpu.SMEM),
        ],
        out_specs=pl.BlockSpec(memory_space=pltpu.VMEM),
        scratch_shapes=[
            pltpu.VMEM((8, BLK), F32),
            pltpu.VMEM((2, 8, BLK), F32),
            pltpu.VMEM((nb, samples, BLK), BF16),
            pltpu.VMEM((nb, half, BLK), BF16),
            pltpu.VMEM((nb, half, BLK), BF16),
            pltpu.VMEM((3, variants, traits), BF16),
            *pair_of(F32, (2,), F32),
            *pair_of(F32, (), F32),
            *pair_of(F32, (), BF16),
            *pair_of(F32, (), BF16),
            *pair_of(BF16, (2,), BF16),
            pltpu.VMEM((variants, traits), F32),
            pltpu.VMEM((variants, traits), F32),
            pltpu.VMEM((variants, traits), F32),
            pltpu.VMEM((2, nb, BLK, traits), BF16),
            pltpu.VMEM((2, nb, BLK, traits), BF16),
            pltpu.VMEM((variants, traits), BF16),
            pltpu.VMEM((BLK, traits), BF16),
            pltpu.VMEM((2, HB // 2, traits), F32),
            pltpu.VMEM((2, HB // 2, traits), BF16),
            pltpu.VMEM((2, HB // 2, traits), BF16),
            dma((nb,)), dma((nb,)),
            dma((nb + len(PARTS),)), dma((nb + len(PARTS),)),
            dma((nb + len(PARTS),)), dma((nb + len(PARTS),)),
            dma((nb,)), dma((nb,)), dma((nb,)), dma((nb,)), dma((2,)), dma((2,)),
            dma((n_groups,)), dma((n_groups,)), dma((n_groups,)), dma((n_groups,)), dma((n_groups,)), dma((n_groups,)),
            dma((2, nb + 1)), dma((2, nb + 1)), dma((nb + 1,)), dma((nb + 1,)), dma((2,)), dma((2,)),
        ],
        compiler_params=pltpu.CompilerParams(
            collective_id=0, has_side_effects=True, vmem_limit_bytes=60 * 1024 * 1024
        ),
        cost_estimate=pl.CostEstimate(
            flops=2 * 20 * BLK * BLK * samples, bytes_accessed=4 * samples * variants, transcendentals=0
        ),
    )(dosage, effects, depth)


def solution(mesh):
    return jax.shard_map(
        functools.partial(body, mesh.shape["genome"], mesh.shape["samp"]),
        mesh=mesh,
        in_specs=(P("samp", "genome"), P("genome", "samp"), P("genome")),
        out_specs=P("genome", "samp"),
        check_vma=False,
    )
```

```python
import functools

import jax
import jax.numpy as jnp
from jax import lax
from jax.experimental import pallas as pl
from jax.experimental.pallas import tpu as pltpu
from jax.sharding import PartitionSpec as P

BLK = 256
HB = BLK // 2
MESH = pl.DeviceIdType.MESH
F32 = jnp.float32
BF16 = jnp.bfloat16
CONTRACT0 = (((0,), (0,)), ((), ()))
PARTS = (2, 4, 8, 8)


def gram(left, right):
    return lax.dot_general(left, right, CONTRACT0, preferred_element_type=F32)


def dot(left, right):
    return jnp.dot(left, right, preferred_element_type=F32)


def make_groups(nb):
    def cols(t):
        return t * BLK, (t + 1) * BLK

    x = [[(t, nb) + cols(t)] for t in range(1, nb)] + [[(0, nb, 0, HB)]]
    z = [[(0, t) + cols(t)] + ([(t - 1, t) + cols(t - 1)] if t > 1 else []) for t in range(1, nb)]
    z += [[(0, 1, 0, HB)]]
    spots = [0, nb * BLK // 2, nb * BLK, (nb + 1) * BLK, (nb + 2) * BLK, (nb + 3) * BLK]
    late = [[(0, 1) + spot] for spot in zip(spots[:-1], spots[1:])]
    return x, z, late


def kernel(
    n_genome, n_samp, nb, half, scale,
    x_ref, e_ref, depth_ref, out_ref,
    d_ref, dep, own, xbuf, zbuf, eff,
    sum_x, sum_z, sum_t, sum_l, cin_x, cin_z, cin_t, cin_l, yo_x, yo_z, yo_t, yo_l, yi_x, yi_z, yi_t, yi_l,
    cor_x, cor_z, cor_t, cor_l,
    acc, par, far, hop_out, hop_in, pair_e, mate_far, last_sum, last_out, last_in,
    own_sem, own_e_sem, x_send, x_recv, z_send, z_recv, ex_send, ex_recv, ez_send, ez_recv, ds_send, ds_recv,
    a_send, a_recv, b_send, b_recv, c_send, c_recv, h_send, h_recv, m_send, m_recv, l_send, l_recv,
):
    g = lax.axis_index("genome")
    s = lax.axis_index("samp")
    q = lax.rem(g, 2)
    sign = 1 - 2 * q
    partner = g + sign
    z_from = g + 2 * sign
    z_to = g - 2 * sign
    has_from = jnp.logical_and(z_from >= 0, z_from < n_genome)
    has_to = jnp.logical_and(z_to >= 0, z_to < n_genome)
    last = nb - 1

    def mine(u):
        return u + q * (nb - 1 - 2 * u)

    def other(u):
        return nb - 1 - mine(u)

    core = lax.rem(s, 2)
    core_mate = s + 1 - 2 * core
    cross_mate = lax.rem(s + 2, n_samp)

    def remote(src, dst, ss, rsem, gg, sss):
        return pltpu.make_async_remote_copy(
            src_ref=src, dst_ref=dst, send_sem=ss, recv_sem=rsem,
            device_id=(gg, sss), device_id_type=MESH,
        )

    def at_block(b):
        return pl.ds(pl.multiple_of(b * BLK, BLK), BLK)

    def half_rows(which, low, high):
        return pl.ds(pl.multiple_of(which * half + low, 16), high - low)

    barrier = pltpu.get_barrier_semaphore()
    for mate in (core_mate, cross_mate):
        pl.semaphore_signal(barrier, inc=1, device_id=(g, mate), device_id_type=MESH)
    for mate in (s, core_mate):
        pl.semaphore_signal(barrier, inc=1, device_id=(partner, mate), device_id_type=MESH)

    @pl.when(has_from)
    def _():
        pl.semaphore_signal(barrier, inc=1, device_id=(z_from, s), device_id_type=MESH)

    @pl.when(has_to)
    def _():
        pl.semaphore_signal(barrier, inc=1, device_id=(z_to, s), device_id_type=MESH)

    own_copies = [
        pltpu.make_async_copy(x_ref.at[:, at_block(mine(u))], own.at[u], own_sem.at[u]) for u in range(nb)
    ]
    own_effects = [
        pltpu.make_async_copy(e_ref.at[at_block(mine(u)), :], eff.at[0, u * BLK : (u + 1) * BLK], own_e_sem.at[u])
        for u in range(nb)
    ]
    for c in own_copies + own_effects:
        c.start()
    for u in range(nb):
        d_ref[u : u + 1, :] = jnp.full((1, BLK), depth_ref[mine(u)].astype(F32))
    pl.semaphore_wait(
        barrier, 4 + has_from.astype(jnp.int32) + has_to.astype(jnp.int32)
    )

    pieces = []
    for part in PARTS:
        low = pieces[-1][1] if pieces else 0
        pieces.append((low, low + half // part))

    def x_part(t, low, high, left, right, n):
        src = pl.ds(pl.multiple_of(other(t) * BLK + left, HB), right - left)
        return remote(
            x_ref.at[half_rows(1 - q, low, high), src], xbuf.at[t, low:high, left:right],
            x_send.at[n], x_recv.at[n], partner, s,
        )

    def z_part(v, low, high, left, right, n):
        src = pl.ds(pl.multiple_of(mine(v) * BLK + left, HB), right - left)
        return remote(
            x_ref.at[half_rows(q, low, high), src], zbuf.at[v, low:high, left:right],
            z_send.at[n], z_recv.at[n], z_to, s,
        )

    x_copies = [x_part(k + 1, 0, half, 0, BLK, k) for k in range(last)] + [x_part(0, 0, half, 0, HB, last)]
    z_copies = [z_part(k, 0, half, 0, BLK, k) for k in range(last)] + [z_part(last, 0, half, 0, HB, last)]
    x_last = [x_part(0, low, high, HB, BLK, nb + n) for n, (low, high) in enumerate(pieces)]
    z_last = [z_part(last, low, high, HB, BLK, nb + n) for n, (low, high) in enumerate(pieces)]
    e_x = [
        remote(e_ref.at[at_block(other(t)), :], eff.at[1, t * BLK : (t + 1) * BLK], ex_send.at[t], ex_recv.at[t], partner, s)
        for t in range(nb)
    ]
    e_z = [
        remote(e_ref.at[at_block(mine(v)), :], eff.at[2, v * BLK : (v + 1) * BLK], ez_send.at[v], ez_recv.at[v], z_to, s)
        for v in range(nb)
    ]
    d_x = remote(d_ref, dep.at[0], ds_send.at[0], ds_recv.at[0], partner, s)
    d_z = remote(d_ref, dep.at[1], ds_send.at[1], ds_recv.at[1], z_to, s)
    e_mate = [
        remote(e_ref.at[at_block(mine(u)), :], pair_e.at[u * BLK : (u + 1) * BLK], m_send.at[u], m_recv.at[u], g, core_mate)
        for u in range(nb)
    ]
    f_mate = remote(eff.at[2, :BLK], mate_far, m_send.at[nb], m_recv.at[nb], g, core_mate)
    to_partner = [d_x] + x_copies + x_last + e_x[::-1]
    to_next = [d_z] + z_copies + z_last + e_z
    for c in to_partner + e_mate:
        c.start()

    @pl.when(has_to)
    def _():
        for c in to_next:
            c.start()

    counter = [0]

    def label(steps, refs):
        out = []
        for step in steps:
            out.append([(counter[0] + n, refs) + gr for n, gr in enumerate(step)])
            counter[0] += len(step)
        return out

    groups_x, groups_z, groups_t = make_groups(nb)
    X = label(groups_x, (sum_x, cin_x, yo_x, yi_x, cor_x))
    Z = label(groups_z, (sum_z, cin_z, yo_z, yi_z, cor_z))
    T = label(groups_t, (sum_t, cin_t, yo_t, yi_t, cor_t))
    late_x, (late_z, late_w, early_w) = [T[0][0], T[1][0]], [step[0] for step in T[2:]]
    SPOT_Z, SPOT_W, SPOT_V = nb * BLK, (nb + 1) * BLK, (nb + 2) * BLK
    L = label([[(0, nb * (nb + 1) // 2, 0, BLK)]], (sum_l, cin_l, yo_l, yi_l, cor_l))[0][0]

    def to_core(group):
        i, (total, cin, _, _, _), low, high, left, right = group
        return remote(
            total.at[low:high, 1 - core, :, left:right], cin.at[low:high, :, left:right],
            a_send.at[i], a_recv.at[i], g, core_mate,
        )

    def to_cross(group):
        i, (_, _, y_out, y_in, _), low, high, left, right = group
        return remote(
            y_out.at[low:high, :, left:right], y_in.at[low:high, :, left:right],
            b_send.at[i], b_recv.at[i], g, cross_mate,
        )

    def share(group):
        i, (_, _, _, _, corr), low, high, left, right = group
        part = corr.at[low:high, core, :, left:right]
        return remote(part, part, c_send.at[i], c_recv.at[i], g, core_mate)

    def stage1(group):
        to_core(group).start()

    def stage2(group):
        i, (total, cin, y_out, _, _), low, high, left, right = group
        to_core(group).wait_recv()
        for a in range(low, high):
            value = total[a, core, :, left:right] + cin[a, :, left:right]
            total[a, core, :, left:right] = value
            y_out[a, :, left:right] = value.astype(y_out.dtype)
        to_cross(group).start()

    def stage3(group):
        i, (total, _, _, y_in, corr), low, high, left, right = group
        to_cross(group).wait_recv()
        for a in range(low, high):
            value = total[a, core, :, left:right] + y_in[a, :, left:right].astype(F32)
            corr[a, core, :, left:right] = value.astype(BF16)
        share(group).start()

    def stage4(group):
        share(group).wait_recv()

    def weight(drow, k, width):
        return jnp.where(drow >= jnp.asarray(k, F32), F32(scale), F32(0.0))[:, :width]

    def row_of(ref, n):
        return ref[pl.ds(n, 1), :]

    def x_weight(t, u, width):
        drow = jnp.where(q == 0, row_of(d_ref, u), row_of(dep.at[0], nb - 1 - t))
        return weight(drow, (nb + t - u), width)

    def z_weight(t, v, width):
        drow = jnp.where(q == 0, row_of(dep.at[0], nb - 1 - t), row_of(dep.at[1], v))
        return weight(drow, (nb + v - t), width)

    def put(ref, a, left, right, value):
        for h in range(2):
            ref[a, h, :, left:right] = value[h * HB : (h + 1) * HB]

    def got(ref, a, left, right):
        return ref[a, :, :, left:right].reshape(BLK, right - left)

    def stack(ref, low, high, left, right):
        return ref[low:high, :, :, left:right].reshape((high - low) * BLK, right - left)

    def block(n):
        return slice(n * BLK, (n + 1) * BLK)

    for c in own_copies + own_effects:
        c.wait()

    def local_row(i, carry):
        def local_pair(j, carry):
            full = gram(own[i, :half], own[j, :half]) + gram(own[i, half:], own[j, half:])
            drow = jnp.where(q == 0, row_of(d_ref, i), row_of(d_ref, j))
            full = full * weight(drow, (j - i).astype(F32), BLK)
            put(sum_l, i * (2 * nb - i + 1) // 2 + (j - i), 0, BLK, full)
            return carry

        return lax.fori_loop(i, nb, local_pair, carry)

    lax.fori_loop(0, nb, local_row, 0)
    stage1(L)
    acc[...] = jnp.zeros_like(acc)
    stage2(L)
    d_x.wait_recv()

    @pl.when(has_from)
    def _():
        d_z.wait_recv()

    def x_grams(t, left, right):
        def pair(u, carry):
            full = gram(own[u, half_rows(q, 0, half), :], xbuf[t, :, left:right])
            put(sum_x, u, t * BLK + left, t * BLK + right, full * x_weight(t, u, right - left))
            return carry

        lax.fori_loop(t, nb, pair, 0)

    def z_grams(low, high, t, left, right):
        def pair(v, carry):
            full = gram(zbuf[v], xbuf[t, :, left:right])
            put(sum_z, v, t * BLK + left, t * BLK + right, full * z_weight(t, v, right - left))
            return carry

        lax.fori_loop(low, high, pair, 0)

    def local_products():
        def local_row(i, carry):
            def local_pair(j, carry):
                corr = got(cor_l, i * (2 * nb - i + 1) // 2 + (j - i), 0, BLK)
                acc[at_block(i), :] += dot(corr, eff[0, at_block(j), :])

                @pl.when(j > i)
                def _():
                    acc[at_block(j), :] += gram(corr, eff[0, at_block(i), :])

                return carry

            return lax.fori_loop(i, nb, local_pair, carry)

        lax.fori_loop(0, nb, local_row, 0)

    def from_groups(k):
        return Z[k] + ([early_w] if k == last else [])

    def both(stage, k):
        for group in X[k]:
            stage(group)

        @pl.when(has_from)
        def _():
            for group in from_groups(k):
                stage(group)

    def par_rows(t):
        par[block(t), :] = gram(stack(cor_x, t, nb, t * BLK, (t + 1) * BLK), eff[0, t * BLK :])

    def finish(groups):
        for group in groups:
            for c in (to_core(group), to_cross(group), share(group)):
                c.wait_send()

    for k in range(nb):
        t, left, right = (k + 1, 0, BLK) if k < last else (0, 0, HB)
        x_copies[k].wait_recv()
        x_grams(t, left, right)
        stage1(X[k][0])

        @pl.when(has_from)
        def _():
            z_copies[k].wait_recv()
            if k < last:
                z_grams(0, t, t, left, right)
                if k:
                    z_grams(k, k + 1, k, left, right)
            else:
                z_grams(0, 1, 0, left, right)
                full = gram(zbuf[last, :, left:right], xbuf[last]) * z_weight(last, last, BLK)
                for h in range(2):
                    sum_t[0, h, :, SPOT_V : SPOT_V + BLK] = full[h * HB // 2 : (h + 1) * HB // 2]
            for group in from_groups(k):
                stage1(group)

        both(stage2, k)
        if k == 1:
            stage3(L)
            both(stage3, 0)
            stage4(L)
            local_products()
            both(stage4, 0)
            par_rows(1)
        if k == 2:
            both(stage3, 1)
            both(stage4, 1)
            par_rows(2)

    for n, (low, high) in enumerate(pieces):
        final = n == len(pieces) - 1

        def add(left, value, factor):
            for h in range(2):
                part = value[h * HB // 2 : (h + 1) * HB // 2]
                if n:
                    part = sum_t[0, h, :, left : left + BLK] + part
                sum_t[0, h, :, left : left + BLK] = part * factor if final else part

        if n == 0:
            for c in e_mate:
                c.wait_recv()
            for c in e_mate + to_partner[:last]:
                c.wait_send()
            finish(sum(X[: last - 1], [L]))

            @pl.when(has_to)
            def _():
                for c in to_next[:last]:
                    c.wait_send()

            @pl.when(has_from)
            def _():
                finish(sum(Z[: last - 1], []))

        if n == 1:
            both(stage3, 2)
        if n == 2:
            both(stage4, 2)
            par_rows(last)
            both(stage3, last)
        if n == 3:
            both(stage4, last)
        x_last[n].wait_recv()
        piece = xbuf[0, low:high, HB:].T

        @pl.when(has_from)
        def _():
            add(SPOT_Z, dot(piece, zbuf[0, low:high]), z_weight(0, 0, BLK) if final else None)
            if final:
                stage1(late_z)
            z_last[n].wait_recv()
            full = dot(zbuf[last, low:high, HB:].T, xbuf[last, low:high])
            add(SPOT_W, full, z_weight(last, last, BLK) if final else None)
            if final:
                stage1(late_w)

        for u in range(nb):
            full = dot(piece, own[u, half_rows(q, low, high), :])
            add(u * BLK, full, x_weight(0, u, BLK) if final else None)
            if final and u % (nb // 2) == nb // 2 - 1:
                stage1(late_x[u // (nb // 2)])

    @pl.when(has_from)
    def _():
        stage2(late_z)
        stage2(late_w)

    for group in late_x:
        stage2(group)

    def hop(n, t, low=0, high=BLK):
        i = nb if low else t
        return remote(
            hop_out.at[n, t, low:high], hop_in.at[n, t, low:high], h_send.at[n, i], h_recv.at[n, i],
            partner if n == 0 else z_from, s,
        )

    hops_x = [hop(0, t) for t in range(1, nb)] + [hop(0, 0, 0, HB)]
    hops_last = [
        remote(last_out.at[n], last_in.at[core], l_send.at[n], l_recv.at[core], partner, to)
        for n, to in enumerate((s, core_mate))
    ]
    last_arrivals = [
        remote(last_out.at[0], last_in.at[n], l_send.at[0], l_recv.at[n], partner, s) for n in range(2)
    ]
    hops_z = [hop(1, v) for v in range(last)] + [hop(1, last, 0, HB), hop(1, last, HB, BLK)]

    def late(left, right):
        return cor_t[0, :, :, left:right].reshape(HB, right - left)

    par[:HB, :] = gram(stack(cor_x, 0, nb, 0, HB), eff[0])

    @pl.when(has_from)
    def _():
        e_z[0].wait_recv()
        f_mate.start()
        par[:HB, :] += gram(got(cor_z, 0, 0, HB), eff[2, block(0)])

    for t in range(1, last):
        @pl.when(has_from)
        def _():
            e_z[t].wait_recv()
            par[block(t), :] += gram(stack(cor_z, 0, t + 1, t * BLK, (t + 1) * BLK), eff[2, : (t + 1) * BLK])

        hop_out[0, t] = par[block(t), :].astype(BF16)
        hops_x[t - 1].start()

    hop_out[0, 0, :HB] = par[:HB, :].astype(BF16)
    hops_x[nb - 1].start()
    e_x[last].wait_recv()

    @pl.when(has_from)
    def _():
        hop_out[1, last, :HB] = dot(late(SPOT_V, SPOT_V + BLK), eff[1, block(last)]).astype(BF16)
        hops_z[last].start()

    for v in range(last - 1, 0, -1):
        e_x[v].wait_recv()

        @pl.when(has_from)
        def _():
            hop_out[1, v] = dot(got(cor_z, v, v * BLK, nb * BLK), eff[1, v * BLK :]).astype(BF16)
            hops_z[v].start()

    @pl.when(has_from)
    def _():
        stage3(late_z)
        par[block(last), :] += gram(stack(cor_z, 0, last, last * BLK, nb * BLK), eff[2, : last * BLK])
        stage3(late_w)
        far[block(0), :] = dot(got(cor_z, 0, BLK, nb * BLK), eff[1, BLK:])

    for u in range(1, nb):
        acc[block(u), :] += dot(got(cor_x, u, BLK, (u + 1) * BLK), eff[1, BLK : (u + 1) * BLK])
    for c in to_partner[last:-1]:
        c.wait_send()
    finish(sum(X[last - 1 :], []))

    @pl.when(has_to)
    def _():
        for c in to_next[last:-1]:
            c.wait_send()

    @pl.when(has_from)
    def _():
        f_mate.wait_send()
        finish(sum(Z[last - 1 :], [early_w]))

    e_x[0].wait_recv()

    @pl.when(has_from)
    def _():
        e_z[last].wait_recv()
        far[block(0), :] += dot(got(cor_z, 0, 0, HB), eff[1, :HB])
        par[block(last), :] += gram(late(SPOT_V, SPOT_V + BLK), eff[2, last * BLK : last * BLK + HB])
        stage4(late_z)
        hop_out[1, 0] = (far[block(0), :] + gram(late(SPOT_Z, SPOT_Z + BLK), eff[1, HB:BLK])).astype(BF16)
        hops_z[0].start()
        stage4(late_w)
        corr = late(SPOT_W, SPOT_W + BLK)
        par[block(last), :] += gram(corr, eff[2, last * BLK + HB :])
        hop_out[1, last, HB:] = dot(corr, eff[1, block(last)]).astype(BF16)
        hops_z[nb].start()

    hop_out[0, last] = par[block(last), :].astype(BF16)
    hops_x[last - 1].start()
    def last_rows(left, right):
        return cor_t[0, core, :, left:right]

    @pl.when(has_from)
    def _():
        f_mate.wait_recv()
        rows = last_rows(SPOT_Z, SPOT_Z + BLK)
        last_sum[0] = dot(rows, eff[2, :BLK])
        last_sum[1] = dot(rows, mate_far[...])

    @pl.when(jnp.logical_not(has_from))
    def _():
        last_sum[...] = jnp.zeros_like(last_sum)

    acc[...] += dot(stack(cor_x, 0, nb, 0, HB), eff[1, :HB])
    middle = nb * BLK // 2
    stage3(late_x[0])
    last_sum[0] += dot(last_rows(0, middle), eff[0, :middle])
    last_sum[1] += dot(last_rows(0, middle), pair_e[:middle])
    stage3(late_x[1])
    for n, effects in enumerate((eff.at[0], pair_e)):
        value = last_sum[n] + dot(last_rows(middle, nb * BLK), effects[middle:])
        last_out[n] = value.astype(BF16)
        hops_last[n].start()

    for group in late_x:
        stage4(group)
    value = gram(late(0, nb * BLK), eff[1, HB:BLK])
    for u in range(nb):
        out_ref[at_block(mine(u)), :] = acc[block(u), :] + value[block(u)]
    to_partner[-1].wait_send()

    @pl.when(has_to)
    def _():
        to_next[-1].wait_send()

    finish(late_x)

    @pl.when(has_from)
    def _():
        finish([late_z, late_w])

    for t in range(1, nb):
        hops_x[t - 1].wait_recv()
        out_ref[at_block(other(t)), :] += hop_in[0, t].astype(F32)

    @pl.when(has_to)
    def _():
        for v in list(range(last - 1, -1, -1)) + [last]:
            hops_z[v].wait_recv()
            if v == last:
                hops_z[nb].wait_recv()
            out_ref[at_block(mine(v)), :] += hop_in[1, v].astype(F32)

    hops_x[nb - 1].wait_recv()
    first = pl.ds(pl.multiple_of(other(0) * BLK, BLK), HB)
    out_ref[first, :] += hop_in[0, 0, :HB].astype(F32)
    for n, c in enumerate(last_arrivals):
        c.wait_recv()
        rows = pl.ds(pl.multiple_of(other(0) * BLK + HB + n * (HB // 2), HB // 2), HB // 2)
        out_ref[rows, :] += last_in[n].astype(F32)
    for c in hops_x + hops_last:
        c.wait_send()

    @pl.when(has_from)
    def _():
        for c in hops_z:
            c.wait_send()


def body(n_genome, n_samp, dosage, effects, depth):
    nb = depth.shape[0]
    samples, variants = dosage.shape
    traits = effects.shape[1]
    half = samples // 2
    dma = pltpu.SemaphoreType.DMA
    pairs = nb * (nb + 1) // 2
    n_groups = 1 + sum(len(step) for steps in make_groups(nb) for step in steps)

    def pair_of(kind, lead, dtype):
        wide = pltpu.VMEM((nb,) + lead + (HB, variants), dtype)
        return [
            wide, wide, pltpu.VMEM((1,) + lead + (HB // 2, (nb + 3) * BLK), dtype), pltpu.VMEM((pairs,) + lead + (HB, BLK), kind),
        ]

    return pl.pallas_call(
        functools.partial(kernel, n_genome, n_samp, nb, half, 1.0 / (samples * n_samp)),
        out_shape=pltpu.VMEM((variants, traits), F32),
        in_specs=[
            pl.BlockSpec(memory_space=pl.ANY),
            pl.BlockSpec(memory_space=pl.ANY),
            pl.BlockSpec(memory_space=pltpu.SMEM),
        ],
        out_specs=pl.BlockSpec(memory_space=pltpu.VMEM),
        scratch_shapes=[
            pltpu.VMEM((8, BLK), F32),
            pltpu.VMEM((2, 8, BLK), F32),
            pltpu.VMEM((nb, samples, BLK), BF16),
            pltpu.VMEM((nb, half, BLK), BF16),
            pltpu.VMEM((nb, half, BLK), BF16),
            pltpu.VMEM((3, variants, traits), BF16),
            *pair_of(F32, (2,), F32),
            *pair_of(F32, (), F32),
            *pair_of(F32, (), BF16),
            *pair_of(F32, (), BF16),
            *pair_of(BF16, (2,), BF16),
            pltpu.VMEM((variants, traits), F32),
            pltpu.VMEM((variants, traits), F32),
            pltpu.VMEM((variants, traits), F32),
            pltpu.VMEM((2, nb, BLK, traits), BF16),
            pltpu.VMEM((2, nb, BLK, traits), BF16),
            pltpu.VMEM((variants, traits), BF16),
            pltpu.VMEM((BLK, traits), BF16),
            pltpu.VMEM((2, HB // 2, traits), F32),
            pltpu.VMEM((2, HB // 2, traits), BF16),
            pltpu.VMEM((2, HB // 2, traits), BF16),
            dma((nb,)), dma((nb,)),
            dma((nb + len(PARTS),)), dma((nb + len(PARTS),)),
            dma((nb + len(PARTS),)), dma((nb + len(PARTS),)),
            dma((nb,)), dma((nb,)), dma((nb,)), dma((nb,)), dma((2,)), dma((2,)),
            dma((n_groups,)), dma((n_groups,)), dma((n_groups,)), dma((n_groups,)), dma((n_groups,)), dma((n_groups,)),
            dma((2, nb + 1)), dma((2, nb + 1)), dma((nb + 1,)), dma((nb + 1,)), dma((2,)), dma((2,)),
        ],
        compiler_params=pltpu.CompilerParams(
            collective_id=0, has_side_effects=True, vmem_limit_bytes=60 * 1024 * 1024
        ),
        cost_estimate=pl.CostEstimate(
            flops=2 * 20 * BLK * BLK * samples, bytes_accessed=4 * samples * variants, transcendentals=0
        ),
    )(dosage, effects, depth)


def solution(mesh):
    return jax.shard_map(
        functools.partial(body, mesh.shape["genome"], mesh.shape["samp"]),
        mesh=mesh,
        in_specs=(P("samp", "genome"), P("genome", "samp"), P("genome")),
        out_specs=P("genome", "samp"),
        check_vma=False,
    )
```

```python
import functools

import jax
import jax.numpy as jnp
from jax import lax
from jax.experimental import pallas as pl
from jax.experimental.pallas import tpu as pltpu
from jax.sharding import PartitionSpec as P

BLK = 256
HB = BLK // 2
MESH = pl.DeviceIdType.MESH
F32 = jnp.float32
BF16 = jnp.bfloat16
CONTRACT0 = (((0,), (0,)), ((), ()))
PARTS = (2, 4, 8, 8)


def gram(left, right):
    return lax.dot_general(left, right, CONTRACT0, preferred_element_type=F32)


def dot(left, right):
    return jnp.dot(left, right, preferred_element_type=F32)


def make_groups(nb):
    def cols(t):
        return t * BLK, (t + 1) * BLK

    x = [[(t, nb) + cols(t)] for t in range(1, nb)] + [[(0, nb, 0, HB)]]
    z = [[(0, t) + cols(t)] + ([(t - 1, t) + cols(t - 1)] if t > 1 else []) for t in range(1, nb)]
    z += [[(0, 1, 0, HB)]]
    spots = [0, nb * BLK // 2, nb * BLK, (nb + 1) * BLK, (nb + 2) * BLK, (nb + 3) * BLK]
    late = [[(0, 1) + spot] for spot in zip(spots[:-1], spots[1:])]
    return x, z, late[-1:] + late[:-1]


def kernel(
    n_genome, n_samp, nb, half, scale,
    x_ref, e_ref, depth_ref, out_ref,
    d_ref, dep, own, xbuf, zbuf, eff,
    sum_x, sum_z, sum_t, sum_l, cin_x, cin_z, cin_t, cin_l, yo_x, yo_z, yo_t, yo_l, yi_x, yi_z, yi_t, yi_l,
    cor_x, cor_z, cor_t, cor_l,
    acc, par, far, hop_out, hop_in, pair_e, mate_far, last_sum, last_out, last_in,
    own_sem, own_e_sem, x_send, x_recv, z_send, z_recv, ex_send, ex_recv, ez_send, ez_recv, ds_send, ds_recv,
    a_send, a_recv, b_send, b_recv, c_send, c_recv, h_send, h_recv, m_send, m_recv, l_send, l_recv,
):
    g = lax.axis_index("genome")
    s = lax.axis_index("samp")
    q = lax.rem(g, 2)
    sign = 1 - 2 * q
    partner = g + sign
    z_from = g + 2 * sign
    z_to = g - 2 * sign
    has_from = jnp.logical_and(z_from >= 0, z_from < n_genome)
    has_to = jnp.logical_and(z_to >= 0, z_to < n_genome)
    last = nb - 1

    def mine(u):
        return u + q * (nb - 1 - 2 * u)

    def other(u):
        return nb - 1 - mine(u)

    core = lax.rem(s, 2)
    core_mate = s + 1 - 2 * core
    cross_mate = lax.rem(s + 2, n_samp)

    def remote(src, dst, ss, rsem, gg, sss):
        return pltpu.make_async_remote_copy(
            src_ref=src, dst_ref=dst, send_sem=ss, recv_sem=rsem,
            device_id=(gg, sss), device_id_type=MESH,
        )

    def at_block(b):
        return pl.ds(pl.multiple_of(b * BLK, BLK), BLK)

    def half_rows(which, low, high):
        return pl.ds(pl.multiple_of(which * half + low, 16), high - low)

    barrier = pltpu.get_barrier_semaphore()
    for mate in (core_mate, cross_mate):
        pl.semaphore_signal(barrier, inc=1, device_id=(g, mate), device_id_type=MESH)
    for mate in (s, core_mate):
        pl.semaphore_signal(barrier, inc=1, device_id=(partner, mate), device_id_type=MESH)

    @pl.when(has_from)
    def _():
        pl.semaphore_signal(barrier, inc=1, device_id=(z_from, s), device_id_type=MESH)

    @pl.when(has_to)
    def _():
        pl.semaphore_signal(barrier, inc=1, device_id=(z_to, s), device_id_type=MESH)

    own_copies = [
        pltpu.make_async_copy(x_ref.at[:, at_block(mine(u))], own.at[u], own_sem.at[0]) for u in range(nb)
    ]
    own_effects = [
        pltpu.make_async_copy(e_ref.at[at_block(mine(u)), :], eff.at[0, u * BLK : (u + 1) * BLK], own_e_sem.at[0])
        for u in range(nb)
    ]
    for c in own_copies + own_effects:
        c.start()
    for u in range(nb):
        d_ref[u : u + 1, :] = jnp.full((1, BLK), depth_ref[mine(u)].astype(F32))
    pl.semaphore_wait(
        barrier, 4 + has_from.astype(jnp.int32) + has_to.astype(jnp.int32)
    )

    pieces = []
    for part in PARTS:
        low = pieces[-1][1] if pieces else 0
        pieces.append((low, low + half // part))

    def x_part(t, low, high, left, right, n):
        src = pl.ds(pl.multiple_of(other(t) * BLK + left, HB), right - left)
        return remote(
            x_ref.at[half_rows(1 - q, low, high), src], xbuf.at[t, low:high, left:right],
            x_send.at[0], x_recv.at[n], partner, s,
        )

    def z_part(v, low, high, left, right, n):
        src = pl.ds(pl.multiple_of(mine(v) * BLK + left, HB), right - left)
        return remote(
            x_ref.at[half_rows(q, low, high), src], zbuf.at[v, low:high, left:right],
            z_send.at[0], z_recv.at[n], z_to, s,
        )

    x_copies = [x_part(k + 1, 0, half, 0, BLK, k) for k in range(last)] + [x_part(0, 0, half, 0, HB, last)]
    z_copies = [z_part(k, 0, half, 0, BLK, k) for k in range(last)] + [z_part(last, 0, half, 0, HB, last)]
    x_last = [x_part(0, low, high, HB, BLK, nb + n) for n, (low, high) in enumerate(pieces)]
    z_last = [z_part(last, low, high, HB, BLK, nb + n) for n, (low, high) in enumerate(pieces)]
    e_x = [
        remote(e_ref.at[at_block(other(t)), :], eff.at[1, t * BLK : (t + 1) * BLK], ex_send.at[0], ex_recv.at[t], partner, s)
        for t in range(nb)
    ]
    e_z = [
        remote(e_ref.at[at_block(mine(v)), :], eff.at[2, v * BLK : (v + 1) * BLK], ez_send.at[0], ez_recv.at[v], z_to, s)
        for v in range(nb)
    ]
    d_x = remote(d_ref, dep.at[0], ds_send.at[0], ds_recv.at[0], partner, s)
    d_z = remote(d_ref, dep.at[1], ds_send.at[1], ds_recv.at[1], z_to, s)
    e_mate = remote(eff.at[0], pair_e, m_send.at[0], m_recv.at[0], g, core_mate)
    f_mate = remote(eff.at[2, :BLK], mate_far, m_send.at[1], m_recv.at[1], g, core_mate)
    to_partner = [d_x] + x_copies + x_last + e_x[::-1]
    to_next = [d_z] + z_copies + z_last + e_z
    for c in to_partner:
        c.start()

    @pl.when(has_to)
    def _():
        for c in to_next:
            c.start()

    counter = [0]

    def label(steps, refs):
        out = []
        for step in steps:
            out.append([(counter[0] + n, refs) + gr for n, gr in enumerate(step)])
            counter[0] += len(step)
        return out

    groups_x, groups_z, groups_t = make_groups(nb)
    X = label(groups_x, (sum_x, cin_x, yo_x, yi_x, cor_x))
    Z = label(groups_z, (sum_z, cin_z, yo_z, yi_z, cor_z))
    T = label(groups_t[:1], (sum_t, cin_t, yo_t, yi_t, cor_t))
    early_w = T[0][0]
    refs_t = early_w[1]
    spots = groups_t[1:]
    late_x = [(X[n][0][0], refs_t) + spots[n][0] for n in range(2)]
    late_z, late_w = [(Z[n][0][0], refs_t) + spots[2 + n][0] for n in range(2)]
    SPOT_Z, SPOT_W, SPOT_V = nb * BLK, (nb + 1) * BLK, (nb + 2) * BLK
    L = label([[(0, nb * (nb + 1) // 2, 0, BLK)]], (sum_l, cin_l, yo_l, yi_l, cor_l))[0][0]

    def to_core(group):
        i, (total, cin, _, _, _), low, high, left, right = group
        return remote(
            total.at[low:high, 1 - core, :, left:right], cin.at[low:high, :, left:right],
            a_send.at[i], a_recv.at[i], g, core_mate,
        )

    def to_cross(group):
        i, (_, _, y_out, y_in, _), low, high, left, right = group
        return remote(
            y_out.at[low:high, :, left:right], y_in.at[low:high, :, left:right],
            b_send.at[i], b_recv.at[i], g, cross_mate,
        )

    def share(group):
        i, (_, _, _, _, corr), low, high, left, right = group
        part = corr.at[low:high, core, :, left:right]
        return remote(part, part, c_send.at[i], c_recv.at[i], g, core_mate)

    def stage1(group):
        to_core(group).start()

    def stage2(group):
        i, (total, cin, y_out, _, _), low, high, left, right = group
        to_core(group).wait_recv()
        for a in range(low, high):
            value = total[a, core, :, left:right] + cin[a, :, left:right]
            total[a, core, :, left:right] = value
            y_out[a, :, left:right] = value.astype(y_out.dtype)
        to_cross(group).start()

    def stage3(group):
        i, (total, _, _, y_in, corr), low, high, left, right = group
        to_cross(group).wait_recv()
        for a in range(low, high):
            value = total[a, core, :, left:right] + y_in[a, :, left:right].astype(F32)
            corr[a, core, :, left:right] = value.astype(BF16)
        share(group).start()

    def stage4(group):
        share(group).wait_recv()

    def weight(drow, k, width):
        return jnp.where(drow >= jnp.asarray(k, F32), F32(scale), F32(0.0))[:, :width]

    def row_of(ref, n):
        return ref[pl.ds(n, 1), :]

    def x_weight(t, u, width):
        drow = jnp.where(q == 0, row_of(d_ref, u), row_of(dep.at[0], nb - 1 - t))
        return weight(drow, (nb + t - u), width)

    def z_weight(t, v, width):
        drow = jnp.where(q == 0, row_of(dep.at[0], nb - 1 - t), row_of(dep.at[1], v))
        return weight(drow, (nb + v - t), width)

    def put(ref, a, left, right, value):
        for h in range(2):
            ref[a, h, :, left:right] = value[h * HB : (h + 1) * HB]

    def got(ref, a, left, right):
        return ref[a, :, :, left:right].reshape(BLK, right - left)

    def stack(ref, low, high, left, right):
        return ref[low:high, :, :, left:right].reshape((high - low) * BLK, right - left)

    def block(n):
        return slice(n * BLK, (n + 1) * BLK)

    pltpu.make_async_copy(eff.at[0], eff.at[0], own_e_sem.at[0]).wait()
    e_mate.start()
    pltpu.make_async_copy(own, own, own_sem.at[0]).wait()

    def local_row(i, carry):
        def local_pair(j, carry):
            full = gram(own[i, :half], own[j, :half]) + gram(own[i, half:], own[j, half:])
            drow = jnp.where(q == 0, row_of(d_ref, i), row_of(d_ref, j))
            full = full * weight(drow, (j - i).astype(F32), BLK)
            put(sum_l, i * (2 * nb - i + 1) // 2 + (j - i), 0, BLK, full)
            return carry

        return lax.fori_loop(i, nb, local_pair, carry)

    lax.fori_loop(0, nb, local_row, 0)
    stage1(L)
    acc[...] = jnp.zeros_like(acc)
    stage2(L)
    d_x.wait_recv()

    @pl.when(has_from)
    def _():
        d_z.wait_recv()

    def x_grams(t, left, right):
        def pair(u, carry):
            full = gram(own[u, half_rows(q, 0, half), :], xbuf[t, :, left:right])
            put(sum_x, u, t * BLK + left, t * BLK + right, full * x_weight(t, u, right - left))
            return carry

        lax.fori_loop(t, nb, pair, 0)

    def z_grams(low, high, t, left, right):
        def pair(v, carry):
            full = gram(zbuf[v], xbuf[t, :, left:right])
            put(sum_z, v, t * BLK + left, t * BLK + right, full * z_weight(t, v, right - left))
            return carry

        lax.fori_loop(low, high, pair, 0)

    def local_products():
        def local_row(i, carry):
            def local_pair(j, carry):
                corr = got(cor_l, i * (2 * nb - i + 1) // 2 + (j - i), 0, BLK)
                acc[at_block(i), :] += dot(corr, eff[0, at_block(j), :])

                @pl.when(j > i)
                def _():
                    acc[at_block(j), :] += gram(corr, eff[0, at_block(i), :])

                return carry

            return lax.fori_loop(i, nb, local_pair, carry)

        lax.fori_loop(0, nb, local_row, 0)

    def from_groups(k):
        return Z[k] + ([early_w] if k == last else [])

    def both(stage, k):
        for group in X[k]:
            stage(group)

        @pl.when(has_from)
        def _():
            for group in from_groups(k):
                stage(group)

    def par_rows(t):
        par[block(t), :] = gram(stack(cor_x, t, nb, t * BLK, (t + 1) * BLK), eff[0, t * BLK :])

    def finish(groups):
        for group in groups:
            for c in (to_core(group), to_cross(group), share(group)):
                c.wait_send()

    for k in range(nb):
        t, left, right = (k + 1, 0, BLK) if k < last else (0, 0, HB)
        x_copies[k].wait_recv()
        x_grams(t, left, right)
        stage1(X[k][0])

        @pl.when(has_from)
        def _():
            z_copies[k].wait_recv()
            if k < last:
                z_grams(0, t, t, left, right)
                if k:
                    z_grams(k, k + 1, k, left, right)
            else:
                z_grams(0, 1, 0, left, right)
                full = gram(zbuf[last, :, left:right], xbuf[last]) * z_weight(last, last, BLK)
                for h in range(2):
                    sum_t[0, h, :, SPOT_V : SPOT_V + BLK] = full[h * HB // 2 : (h + 1) * HB // 2]
            for group in from_groups(k):
                stage1(group)

        both(stage2, k)
        if k == 1:
            stage3(L)
            both(stage3, 0)
            stage4(L)
            local_products()
            both(stage4, 0)
            par_rows(1)
        if k == 2:
            both(stage3, 1)
            both(stage4, 1)
            par_rows(2)

    for n, (low, high) in enumerate(pieces):
        final = n == len(pieces) - 1

        def add(left, value, factor):
            for h in range(2):
                part = value[h * HB // 2 : (h + 1) * HB // 2]
                if n:
                    part = sum_t[0, h, :, left : left + BLK] + part
                sum_t[0, h, :, left : left + BLK] = part * factor if final else part

        if n == 0:
            e_mate.wait()
            finish(sum(X[: last - 1], [L]))

            @pl.when(has_from)
            def _():
                finish(sum(Z[: last - 1], []))

        if n == 1:
            both(stage3, 2)
        if n == 2:
            both(stage4, 2)
            par_rows(last)
            both(stage3, last)
        if n == 3:
            both(stage4, last)
        x_last[n].wait_recv()
        piece = xbuf[0, low:high, HB:].T

        @pl.when(has_from)
        def _():
            add(SPOT_Z, dot(piece, zbuf[0, low:high]), z_weight(0, 0, BLK) if final else None)
            if final:
                stage1(late_z)
            z_last[n].wait_recv()
            full = dot(zbuf[last, low:high, HB:].T, xbuf[last, low:high])
            add(SPOT_W, full, z_weight(last, last, BLK) if final else None)
            if final:
                stage1(late_w)

        for u in range(nb):
            full = dot(piece, own[u, half_rows(q, low, high), :])
            add(u * BLK, full, x_weight(0, u, BLK) if final else None)
            if final and u % (nb // 2) == nb // 2 - 1:
                stage1(late_x[u // (nb // 2)])

    @pl.when(has_from)
    def _():
        stage2(late_z)
        stage2(late_w)

    for group in late_x:
        stage2(group)

    def hop(n, t, low=0, high=BLK):
        i = nb if low else t
        return remote(
            hop_out.at[n, t, low:high], hop_in.at[n, t, low:high], h_send.at[n, i], h_recv.at[n, i],
            partner if n == 0 else z_from, s,
        )

    hops_x = [hop(0, t) for t in range(1, nb)] + [hop(0, 0, 0, HB)]
    hops_last = [
        remote(last_out.at[n], last_in.at[core], l_send.at[n], l_recv.at[core], partner, to)
        for n, to in enumerate((s, core_mate))
    ]
    last_arrivals = [
        remote(last_out.at[0], last_in.at[n], l_send.at[0], l_recv.at[n], partner, s) for n in range(2)
    ]
    hops_z = [hop(1, v) for v in range(last)] + [hop(1, last, 0, HB), hop(1, last, HB, BLK)]

    def late(left, right):
        return cor_t[0, :, :, left:right].reshape(HB, right - left)

    par[:HB, :] = gram(stack(cor_x, 0, nb, 0, HB), eff[0])

    @pl.when(has_from)
    def _():
        e_z[0].wait_recv()
        f_mate.start()
        par[:HB, :] += gram(got(cor_z, 0, 0, HB), eff[2, block(0)])

    for t in range(1, last):
        @pl.when(has_from)
        def _():
            e_z[t].wait_recv()
            par[block(t), :] += gram(stack(cor_z, 0, t + 1, t * BLK, (t + 1) * BLK), eff[2, : (t + 1) * BLK])

        hop_out[0, t] = par[block(t), :].astype(BF16)
        hops_x[t - 1].start()

    hop_out[0, 0, :HB] = par[:HB, :].astype(BF16)
    hops_x[nb - 1].start()
    e_x[last].wait_recv()

    @pl.when(has_from)
    def _():
        hop_out[1, last, :HB] = dot(late(SPOT_V, SPOT_V + BLK), eff[1, block(last)]).astype(BF16)
        hops_z[last].start()

    for v in range(last - 1, 0, -1):
        e_x[v].wait_recv()

        @pl.when(has_from)
        def _():
            hop_out[1, v] = dot(got(cor_z, v, v * BLK, nb * BLK), eff[1, v * BLK :]).astype(BF16)
            hops_z[v].start()

    @pl.when(has_from)
    def _():
        stage3(late_z)
        par[block(last), :] += gram(stack(cor_z, 0, last, last * BLK, nb * BLK), eff[2, : last * BLK])
        stage3(late_w)
        far[block(0), :] = dot(got(cor_z, 0, BLK, nb * BLK), eff[1, BLK:])

    for u in range(1, nb):
        acc[block(u), :] += dot(got(cor_x, u, BLK, (u + 1) * BLK), eff[1, BLK : (u + 1) * BLK])
    d_x.wait_send()
    remote(xbuf, xbuf, x_send.at[0], x_recv.at[0], partner, s).wait_send()
    finish(sum(X[last - 1 :], []))

    @pl.when(has_to)
    def _():
        d_z.wait_send()
        remote(zbuf, zbuf, z_send.at[0], z_recv.at[0], z_to, s).wait_send()

    @pl.when(has_from)
    def _():
        f_mate.wait_send()
        finish(sum(Z[last - 1 :], [early_w]))

    e_x[0].wait_recv()

    @pl.when(has_from)
    def _():
        e_z[last].wait_recv()
        far[block(0), :] += dot(got(cor_z, 0, 0, HB), eff[1, :HB])
        par[block(last), :] += gram(late(SPOT_V, SPOT_V + BLK), eff[2, last * BLK : last * BLK + HB])
        stage4(late_z)
        hop_out[1, 0] = (far[block(0), :] + gram(late(SPOT_Z, SPOT_Z + BLK), eff[1, HB:BLK])).astype(BF16)
        hops_z[0].start()
        stage4(late_w)
        corr = late(SPOT_W, SPOT_W + BLK)
        par[block(last), :] += gram(corr, eff[2, last * BLK + HB :])
        hop_out[1, last, HB:] = dot(corr, eff[1, block(last)]).astype(BF16)
        hops_z[nb].start()

    hop_out[0, last] = par[block(last), :].astype(BF16)
    hops_x[last - 1].start()
    def last_rows(left, right):
        return cor_t[0, core, :, left:right]

    @pl.when(has_from)
    def _():
        f_mate.wait_recv()
        rows = last_rows(SPOT_Z, SPOT_Z + BLK)
        last_sum[0] = dot(rows, eff[2, :BLK])
        last_sum[1] = dot(rows, mate_far[...])

    @pl.when(jnp.logical_not(has_from))
    def _():
        last_sum[...] = jnp.zeros_like(last_sum)

    acc[...] += dot(stack(cor_x, 0, nb, 0, HB), eff[1, :HB])
    middle = nb * BLK // 2
    stage3(late_x[0])
    last_sum[0] += dot(last_rows(0, middle), eff[0, :middle])
    last_sum[1] += dot(last_rows(0, middle), pair_e[:middle])
    stage3(late_x[1])
    for n, effects in enumerate((eff.at[0], pair_e)):
        value = last_sum[n] + dot(last_rows(middle, nb * BLK), effects[middle:])
        last_out[n] = value.astype(BF16)
        hops_last[n].start()

    for group in late_x:
        stage4(group)
    value = gram(late(0, nb * BLK), eff[1, HB:BLK])
    for u in range(nb):
        out_ref[at_block(mine(u)), :] = acc[block(u), :] + value[block(u)]
    remote(eff.at[1], eff.at[1], ex_send.at[0], ex_recv.at[0], partner, s).wait_send()

    @pl.when(has_to)
    def _():
        remote(eff.at[2], eff.at[2], ez_send.at[0], ez_recv.at[0], z_to, s).wait_send()

    finish(late_x)

    @pl.when(has_from)
    def _():
        finish([late_z, late_w])

    for t in range(1, nb):
        hops_x[t - 1].wait_recv()
        out_ref[at_block(other(t)), :] += hop_in[0, t].astype(F32)

    @pl.when(has_to)
    def _():
        for v in list(range(last - 1, -1, -1)) + [last]:
            hops_z[v].wait_recv()
            if v == last:
                hops_z[nb].wait_recv()
            out_ref[at_block(mine(v)), :] += hop_in[1, v].astype(F32)

    hops_x[nb - 1].wait_recv()
    first = pl.ds(pl.multiple_of(other(0) * BLK, BLK), HB)
    out_ref[first, :] += hop_in[0, 0, :HB].astype(F32)
    for n, c in enumerate(last_arrivals):
        c.wait_recv()
        rows = pl.ds(pl.multiple_of(other(0) * BLK + HB + n * (HB // 2), HB // 2), HB // 2)
        out_ref[rows, :] += last_in[n].astype(F32)
    for c in hops_x + hops_last:
        c.wait_send()

    @pl.when(has_from)
    def _():
        for c in hops_z:
            c.wait_send()


def body(n_genome, n_samp, dosage, effects, depth):
    nb = depth.shape[0]
    samples, variants = dosage.shape
    traits = effects.shape[1]
    half = samples // 2
    dma = pltpu.SemaphoreType.DMA
    pairs = nb * (nb + 1) // 2
    n_groups = 2 + sum(len(step) for steps in make_groups(nb)[:2] for step in steps)

    def pair_of(kind, lead, dtype):
        wide = pltpu.VMEM((nb,) + lead + (HB, variants), dtype)
        return [
            wide, wide, pltpu.VMEM((1,) + lead + (HB // 2, (nb + 3) * BLK), dtype), pltpu.VMEM((pairs,) + lead + (HB, BLK), kind),
        ]

    return pl.pallas_call(
        functools.partial(kernel, n_genome, n_samp, nb, half, 1.0 / (samples * n_samp)),
        out_shape=pltpu.VMEM((variants, traits), F32),
        in_specs=[
            pl.BlockSpec(memory_space=pl.ANY),
            pl.BlockSpec(memory_space=pl.ANY),
            pl.BlockSpec(memory_space=pltpu.SMEM),
        ],
        out_specs=pl.BlockSpec(memory_space=pltpu.VMEM),
        scratch_shapes=[
            pltpu.VMEM((8, BLK), F32),
            pltpu.VMEM((2, 8, BLK), F32),
            pltpu.VMEM((nb, samples, BLK), BF16),
            pltpu.VMEM((nb, half, BLK), BF16),
            pltpu.VMEM((nb, half, BLK), BF16),
            pltpu.VMEM((3, variants, traits), BF16),
            *pair_of(F32, (2,), F32),
            *pair_of(F32, (), F32),
            *pair_of(F32, (), BF16),
            *pair_of(F32, (), BF16),
            *pair_of(BF16, (2,), BF16),
            pltpu.VMEM((variants, traits), F32),
            pltpu.VMEM((variants, traits), F32),
            pltpu.VMEM((variants, traits), F32),
            pltpu.VMEM((2, nb, BLK, traits), BF16),
            pltpu.VMEM((2, nb, BLK, traits), BF16),
            pltpu.VMEM((variants, traits), BF16),
            pltpu.VMEM((BLK, traits), BF16),
            pltpu.VMEM((2, HB // 2, traits), F32),
            pltpu.VMEM((2, HB // 2, traits), BF16),
            pltpu.VMEM((2, HB // 2, traits), BF16),
            dma((1,)), dma((1,)),
            dma((1,)), dma((nb + len(PARTS),)),
            dma((1,)), dma((nb + len(PARTS),)),
            dma((1,)), dma((nb,)), dma((1,)), dma((nb,)), dma((2,)), dma((2,)),
            dma((n_groups,)), dma((n_groups,)), dma((n_groups,)), dma((n_groups,)), dma((n_groups,)), dma((n_groups,)),
            dma((2, nb + 1)), dma((2, nb + 1)), dma((2,)), dma((2,)), dma((2,)), dma((2,)),
        ],
        compiler_params=pltpu.CompilerParams(
            collective_id=0, has_side_effects=True, vmem_limit_bytes=60 * 1024 * 1024
        ),
        cost_estimate=pl.CostEstimate(
            flops=2 * 20 * BLK * BLK * samples, bytes_accessed=4 * samples * variants, transcendentals=0
        ),
    )(dosage, effects, depth)


def solution(mesh):
    return jax.shard_map(
        functools.partial(body, mesh.shape["genome"], mesh.shape["samp"]),
        mesh=mesh,
        in_specs=(P("samp", "genome"), P("genome", "samp"), P("genome")),
        out_specs=P("genome", "samp"),
        check_vma=False,
    )
```

```python
import functools

import jax
import jax.numpy as jnp
from jax import lax
from jax.experimental import pallas as pl
from jax.experimental.pallas import tpu as pltpu
from jax.sharding import PartitionSpec as P

BLK = 256
HB = BLK // 2
MESH = pl.DeviceIdType.MESH
F32 = jnp.float32
BF16 = jnp.bfloat16
CONTRACT0 = (((0,), (0,)), ((), ()))
PARTS = (2, 4, 8, 8)


def gram(left, right):
    return lax.dot_general(left, right, CONTRACT0, preferred_element_type=F32)


def dot(left, right):
    return jnp.dot(left, right, preferred_element_type=F32)


def make_groups(nb):
    def cols(t):
        return t * BLK, (t + 1) * BLK

    x = [[(t, nb) + cols(t)] for t in range(1, nb)] + [[(0, nb, 0, HB)]]
    z = [[(0, t) + cols(t)] + ([(t - 1, t) + cols(t - 1)] if t > 1 else []) for t in range(1, nb)]
    z += [[(0, 1, 0, HB)]]
    spots = [0, nb * BLK // 2, nb * BLK, (nb + 1) * BLK, (nb + 2) * BLK, (nb + 3) * BLK]
    late = [[(0, 1) + spot] for spot in zip(spots[:-1], spots[1:])]
    return x, z, late[-1:] + late[:-1]


def kernel(
    n_genome, n_samp, nb, half, scale,
    x_ref, e_ref, depth_ref, out_ref,
    d_ref, dep, own, xbuf, zbuf, eff,
    sum_x, sum_z, sum_t, sum_l, cin_x, cin_z, cin_t, cin_l, yo_x, yo_z, yo_t, yo_l, yi_x, yi_z, yi_t, yi_l,
    cor_x, cor_z, cor_t, cor_l,
    acc, par, far, hop_out, hop_in, pair_e, mate_far, last_sum, last_out, last_in,
    own_sem, own_e_sem, x_send, x_recv, z_send, z_recv, ex_send, ex_recv, ez_send, ez_recv, ds_send, ds_recv,
    a_send, a_recv, b_send, b_recv, c_send, c_recv, h_send, h_recv, m_send, m_recv, l_send, l_recv,
):
    g = lax.axis_index("genome")
    s = lax.axis_index("samp")
    q = lax.rem(g, 2)
    sign = 1 - 2 * q
    partner = g + sign
    z_from = g + 2 * sign
    z_to = g - 2 * sign
    has_from = jnp.logical_and(z_from >= 0, z_from < n_genome)
    has_to = jnp.logical_and(z_to >= 0, z_to < n_genome)
    last = nb - 1

    def mine(u):
        return u + q * (nb - 1 - 2 * u)

    def other(u):
        return nb - 1 - mine(u)

    core = lax.rem(s, 2)
    core_mate = s + 1 - 2 * core
    cross_mate = lax.rem(s + 2, n_samp)

    def remote(src, dst, ss, rsem, gg, sss):
        return pltpu.make_async_remote_copy(
            src_ref=src, dst_ref=dst, send_sem=ss, recv_sem=rsem,
            device_id=(gg, sss), device_id_type=MESH,
        )

    def at_block(b):
        return pl.ds(pl.multiple_of(b * BLK, BLK), BLK)

    def half_rows(which, low, high):
        return pl.ds(pl.multiple_of(which * half + low, 16), high - low)

    barrier = pltpu.get_barrier_semaphore()
    for mate in (s, core_mate):
        pl.semaphore_signal(barrier, inc=1, device_id=(partner, mate), device_id_type=MESH)

    for mate in (core_mate, cross_mate):
        pl.semaphore_signal(barrier, inc=1, device_id=(g, mate), device_id_type=MESH)
    @pl.when(has_from)
    def _():
        pl.semaphore_signal(barrier, inc=1, device_id=(z_from, s), device_id_type=MESH)

    @pl.when(has_to)
    def _():
        pl.semaphore_signal(barrier, inc=1, device_id=(z_to, s), device_id_type=MESH)

    own_copies = [
        pltpu.make_async_copy(x_ref.at[:, at_block(mine(u))], own.at[u], own_sem.at[0]) for u in range(nb)
    ]
    own_effects = [
        pltpu.make_async_copy(e_ref.at[at_block(mine(u)), :], eff.at[0, u * BLK : (u + 1) * BLK], own_e_sem.at[0])
        for u in range(nb)
    ]
    for c in own_copies + own_effects:
        c.start()
    for u in range(nb):
        d_ref[u : u + 1, :] = jnp.full((1, BLK), depth_ref[mine(u)].astype(F32))
    pl.semaphore_wait(
        barrier, 4 + has_from.astype(jnp.int32) + has_to.astype(jnp.int32)
    )

    pieces = []
    for part in PARTS:
        low = pieces[-1][1] if pieces else 0
        pieces.append((low, low + half // part))

    def x_part(t, low, high, left, right, n):
        src = pl.ds(pl.multiple_of(other(t) * BLK + left, HB), right - left)
        return remote(
            x_ref.at[half_rows(1 - q, low, high), src], xbuf.at[t, low:high, left:right],
            x_send.at[0], x_recv.at[n], partner, s,
        )

    def z_part(v, low, high, left, right, n):
        src = pl.ds(pl.multiple_of(mine(v) * BLK + left, HB), right - left)
        return remote(
            x_ref.at[half_rows(q, low, high), src], zbuf.at[v, low:high, left:right],
            z_send.at[0], z_recv.at[n], z_to, s,
        )

    x_copies = [x_part(k + 1, 0, half, 0, BLK, k) for k in range(last)] + [x_part(0, 0, half, 0, HB, last)]
    z_copies = [z_part(k, 0, half, 0, BLK, k) for k in range(last)] + [z_part(last, 0, half, 0, HB, last)]
    x_last = [x_part(0, low, high, HB, BLK, nb + n) for n, (low, high) in enumerate(pieces)]
    z_last = [z_part(last, low, high, HB, BLK, nb + n) for n, (low, high) in enumerate(pieces)]
    e_x = [
        remote(e_ref.at[at_block(other(t)), :], eff.at[1, t * BLK : (t + 1) * BLK], ex_send.at[0], ex_recv.at[t], partner, s)
        for t in range(nb)
    ]
    e_z = [
        remote(e_ref.at[at_block(mine(v)), :], eff.at[2, v * BLK : (v + 1) * BLK], ez_send.at[0], ez_recv.at[v], z_to, s)
        for v in range(nb)
    ]
    d_x = remote(d_ref, dep.at[0], ds_send.at[0], ds_recv.at[0], partner, s)
    d_z = remote(d_ref, dep.at[1], ds_send.at[1], ds_recv.at[1], z_to, s)
    e_mate = remote(eff.at[0], pair_e, m_send.at[0], m_recv.at[0], g, core_mate)
    f_mate = remote(eff.at[2, :BLK], mate_far, m_send.at[1], m_recv.at[1], g, core_mate)
    to_partner = [d_x] + x_copies + x_last + e_x[::-1]
    to_next = [d_z] + z_copies + z_last + e_z
    for c in to_partner:
        c.start()

    @pl.when(has_to)
    def _():
        for c in to_next:
            c.start()

    counter = [0]

    def label(steps, refs):
        out = []
        for step in steps:
            out.append([(counter[0] + n, refs) + gr for n, gr in enumerate(step)])
            counter[0] += len(step)
        return out

    groups_x, groups_z, groups_t = make_groups(nb)
    X = label(groups_x, (sum_x, cin_x, yo_x, yi_x, cor_x))
    Z = label(groups_z, (sum_z, cin_z, yo_z, yi_z, cor_z))
    T = label(groups_t[:1], (sum_t, cin_t, yo_t, yi_t, cor_t))
    early_w = T[0][0]
    refs_t = early_w[1]
    spots = groups_t[1:]
    late_x = [(X[n][0][0], refs_t) + spots[n][0] for n in range(2)]
    late_z, late_w = [(Z[n][0][0], refs_t) + spots[2 + n][0] for n in range(2)]
    SPOT_Z, SPOT_W, SPOT_V = nb * BLK, (nb + 1) * BLK, (nb + 2) * BLK
    L = label([[(0, nb * (nb + 1) // 2, 0, BLK)]], (sum_l, cin_l, yo_l, yi_l, cor_l))[0][0]

    def to_core(group):
        i, (total, cin, _, _, _), low, high, left, right = group
        return remote(
            total.at[low:high, 1 - core, :, left:right], cin.at[low:high, :, left:right],
            a_send.at[i], a_recv.at[i], g, core_mate,
        )

    def to_cross(group):
        i, (_, _, y_out, y_in, _), low, high, left, right = group
        return remote(
            y_out.at[low:high, :, left:right], y_in.at[low:high, :, left:right],
            b_send.at[i], b_recv.at[i], g, cross_mate,
        )

    def share(group):
        i, (_, _, _, _, corr), low, high, left, right = group
        part = corr.at[low:high, core, :, left:right]
        return remote(part, part, c_send.at[i], c_recv.at[i], g, core_mate)

    def stage1(group):
        to_core(group).start()

    def stage2(group):
        i, (total, cin, y_out, _, _), low, high, left, right = group
        to_core(group).wait_recv()
        for a in range(low, high):
            value = total[a, core, :, left:right] + cin[a, :, left:right]
            total[a, core, :, left:right] = value
            y_out[a, :, left:right] = value.astype(y_out.dtype)
        to_cross(group).start()

    def stage3(group):
        i, (total, _, _, y_in, corr), low, high, left, right = group
        to_cross(group).wait_recv()
        for a in range(low, high):
            value = total[a, core, :, left:right] + y_in[a, :, left:right].astype(F32)
            corr[a, core, :, left:right] = value.astype(BF16)
        share(group).start()

    def stage4(group):
        share(group).wait_recv()

    def weight(drow, k, width):
        return jnp.where(drow >= jnp.asarray(k, F32), F32(scale), F32(0.0))[:, :width]

    def row_of(ref, n):
        return ref[pl.ds(n, 1), :]

    def x_weight(t, u, width):
        drow = jnp.where(q == 0, row_of(d_ref, u), row_of(dep.at[0], nb - 1 - t))
        return weight(drow, (nb + t - u), width)

    def z_weight(t, v, width):
        drow = jnp.where(q == 0, row_of(dep.at[0], nb - 1 - t), row_of(dep.at[1], v))
        return weight(drow, (nb + v - t), width)

    def put(ref, a, left, right, value):
        for h in range(2):
            ref[a, h, :, left:right] = value[h * HB : (h + 1) * HB]

    def got(ref, a, left, right):
        return ref[a, :, :, left:right].reshape(BLK, right - left)

    def stack(ref, low, high, left, right):
        return ref[low:high, :, :, left:right].reshape((high - low) * BLK, right - left)

    def block(n):
        return slice(n * BLK, (n + 1) * BLK)

    pltpu.make_async_copy(eff.at[0], eff.at[0], own_e_sem.at[0]).wait()
    e_mate.start()
    pltpu.make_async_copy(own, own, own_sem.at[0]).wait()

    def local_row(i, carry):
        def local_pair(j, carry):
            full = gram(own[i, :half], own[j, :half]) + gram(own[i, half:], own[j, half:])
            drow = jnp.where(q == 0, row_of(d_ref, i), row_of(d_ref, j))
            full = full * weight(drow, (j - i).astype(F32), BLK)
            put(sum_l, i * (2 * nb - i + 1) // 2 + (j - i), 0, BLK, full)
            return carry

        return lax.fori_loop(i, nb, local_pair, carry)

    lax.fori_loop(0, nb, local_row, 0)
    stage1(L)
    acc[...] = jnp.zeros_like(acc)
    stage2(L)
    d_x.wait_recv()

    @pl.when(has_from)
    def _():
        d_z.wait_recv()

    def x_grams(t, left, right):
        def pair(u, carry):
            full = gram(own[u, half_rows(q, 0, half), :], xbuf[t, :, left:right])
            put(sum_x, u, t * BLK + left, t * BLK + right, full * x_weight(t, u, right - left))
            return carry

        lax.fori_loop(t, nb, pair, 0)

    def z_grams(low, high, t, left, right):
        def pair(v, carry):
            full = gram(zbuf[v], xbuf[t, :, left:right])
            put(sum_z, v, t * BLK + left, t * BLK + right, full * z_weight(t, v, right - left))
            return carry

        lax.fori_loop(low, high, pair, 0)

    def local_products():
        def local_row(i, carry):
            def local_pair(j, carry):
                corr = got(cor_l, i * (2 * nb - i + 1) // 2 + (j - i), 0, BLK)
                acc[at_block(i), :] += dot(corr, eff[0, at_block(j), :])

                @pl.when(j > i)
                def _():
                    acc[at_block(j), :] += gram(corr, eff[0, at_block(i), :])

                return carry

            return lax.fori_loop(i, nb, local_pair, carry)

        lax.fori_loop(0, nb, local_row, 0)

    def from_groups(k):
        return Z[k] + ([early_w] if k == last else [])

    def both(stage, k):
        for group in X[k]:
            stage(group)

        @pl.when(has_from)
        def _():
            for group in from_groups(k):
                stage(group)

    def par_rows(t):
        par[block(t), :] = gram(stack(cor_x, t, nb, t * BLK, (t + 1) * BLK), eff[0, t * BLK :])

    def finish(groups):
        for group in groups:
            for c in (to_core(group), to_cross(group), share(group)):
                c.wait_send()

    for k in range(nb):
        t, left, right = (k + 1, 0, BLK) if k < last else (0, 0, HB)
        x_copies[k].wait_recv()
        x_grams(t, left, right)
        stage1(X[k][0])

        @pl.when(has_from)
        def _():
            z_copies[k].wait_recv()
            if k < last:
                z_grams(0, t, t, left, right)
                if k:
                    z_grams(k, k + 1, k, left, right)
            else:
                z_grams(0, 1, 0, left, right)
                full = gram(zbuf[last, :, left:right], xbuf[last]) * z_weight(last, last, BLK)
                for h in range(2):
                    sum_t[0, h, :, SPOT_V : SPOT_V + BLK] = full[h * HB // 2 : (h + 1) * HB // 2]
            for group in from_groups(k):
                stage1(group)

        both(stage2, k)
        if k == 1:
            stage3(L)
            both(stage3, 0)
            stage4(L)
            local_products()
            both(stage4, 0)
            par_rows(1)
        if k == 2:
            both(stage3, 1)
            both(stage4, 1)
            par_rows(2)

    for n, (low, high) in enumerate(pieces):
        final = n == len(pieces) - 1

        def add(left, value, factor):
            for h in range(2):
                part = value[h * HB // 2 : (h + 1) * HB // 2]
                if n:
                    part = sum_t[0, h, :, left : left + BLK] + part
                sum_t[0, h, :, left : left + BLK] = part * factor if final else part

        if n == 0:
            e_mate.wait()
            finish(sum(X[: last - 1], [L]))

            @pl.when(has_from)
            def _():
                finish(sum(Z[: last - 1], []))

        if n == 1:
            both(stage3, 2)
        if n == 2:
            both(stage4, 2)
            par_rows(last)
            both(stage3, last)
        if n == 3:
            both(stage4, last)
        x_last[n].wait_recv()
        piece = xbuf[0, low:high, HB:].T

        @pl.when(has_from)
        def _():
            add(SPOT_Z, dot(piece, zbuf[0, low:high]), z_weight(0, 0, BLK) if final else None)
            if final:
                stage1(late_z)
            z_last[n].wait_recv()
            full = dot(zbuf[last, low:high, HB:].T, xbuf[last, low:high])
            add(SPOT_W, full, z_weight(last, last, BLK) if final else None)
            if final:
                stage1(late_w)

        for u in range(nb):
            full = dot(piece, own[u, half_rows(q, low, high), :])
            add(u * BLK, full, x_weight(0, u, BLK) if final else None)
            if final and u % (nb // 2) == nb // 2 - 1:
                stage1(late_x[u // (nb // 2)])

    @pl.when(has_from)
    def _():
        stage2(late_z)
        stage2(late_w)

    for group in late_x:
        stage2(group)

    def hop(n, t, low=0, high=BLK):
        i = nb if low else t
        return remote(
            hop_out.at[n, t, low:high], hop_in.at[n, t, low:high], h_send.at[n, i if n == 0 else 0], h_recv.at[n, i],
            partner if n == 0 else z_from, s,
        )

    hops_x = [hop(0, t) for t in range(1, nb)] + [hop(0, 0, 0, HB)]
    hops_last = [
        remote(last_out.at[n], last_in.at[core], l_send.at[n], l_recv.at[core], partner, to)
        for n, to in enumerate((s, core_mate))
    ]
    last_arrivals = [
        remote(last_out.at[0], last_in.at[n], l_send.at[0], l_recv.at[n], partner, s) for n in range(2)
    ]
    hops_z = [hop(1, v) for v in range(last)] + [hop(1, last, 0, HB), hop(1, last, HB, BLK)]

    def late(left, right):
        return cor_t[0, :, :, left:right].reshape(HB, right - left)

    par[:HB, :] = gram(stack(cor_x, 0, nb, 0, HB), eff[0])

    @pl.when(has_from)
    def _():
        e_z[0].wait_recv()
        f_mate.start()
        par[:HB, :] += gram(got(cor_z, 0, 0, HB), eff[2, block(0)])

    for t in range(1, last):
        @pl.when(has_from)
        def _():
            e_z[t].wait_recv()
            par[block(t), :] += gram(stack(cor_z, 0, t + 1, t * BLK, (t + 1) * BLK), eff[2, : (t + 1) * BLK])

        hop_out[0, t] = par[block(t), :].astype(BF16)
        hops_x[t - 1].start()

    hop_out[0, 0, :HB] = par[:HB, :].astype(BF16)
    hops_x[nb - 1].start()
    e_x[last].wait_recv()

    @pl.when(has_from)
    def _():
        hop_out[1, last, :HB] = dot(late(SPOT_V, SPOT_V + BLK), eff[1, block(last)]).astype(BF16)
        hops_z[last].start()

    for v in range(last - 1, 0, -1):
        e_x[v].wait_recv()

        @pl.when(has_from)
        def _():
            hop_out[1, v] = dot(got(cor_z, v, v * BLK, nb * BLK), eff[1, v * BLK :]).astype(BF16)
            hops_z[v].start()

    @pl.when(has_from)
    def _():
        stage3(late_z)
        par[block(last), :] += gram(stack(cor_z, 0, last, last * BLK, nb * BLK), eff[2, : last * BLK])
        stage3(late_w)
        far[block(0), :] = dot(got(cor_z, 0, BLK, nb * BLK), eff[1, BLK:])

    for u in range(1, nb):
        acc[block(u), :] += dot(got(cor_x, u, BLK, (u + 1) * BLK), eff[1, BLK : (u + 1) * BLK])
    d_x.wait_send()
    remote(xbuf, xbuf, x_send.at[0], x_recv.at[0], partner, s).wait_send()
    finish(sum(X[last - 1 :], []))

    @pl.when(has_to)
    def _():
        d_z.wait_send()
        remote(zbuf, zbuf, z_send.at[0], z_recv.at[0], z_to, s).wait_send()

    @pl.when(has_from)
    def _():
        f_mate.wait_send()
        finish(sum(Z[last - 1 :], [early_w]))

    e_x[0].wait_recv()

    @pl.when(has_from)
    def _():
        e_z[last].wait_recv()
        far[block(0), :] += dot(got(cor_z, 0, 0, HB), eff[1, :HB])
        par[block(last), :] += gram(late(SPOT_V, SPOT_V + BLK), eff[2, last * BLK : last * BLK + HB])
        stage4(late_z)
        hop_out[1, 0] = (far[block(0), :] + gram(late(SPOT_Z, SPOT_Z + BLK), eff[1, HB:BLK])).astype(BF16)
        hops_z[0].start()
        stage4(late_w)
        corr = late(SPOT_W, SPOT_W + BLK)
        par[block(last), :] += gram(corr, eff[2, last * BLK + HB :])
        hop_out[1, last, HB:] = dot(corr, eff[1, block(last)]).astype(BF16)
        hops_z[nb].start()

    hop_out[0, last] = par[block(last), :].astype(BF16)
    hops_x[last - 1].start()
    def last_rows(left, right):
        return cor_t[0, core, :, left:right]

    @pl.when(has_from)
    def _():
        f_mate.wait_recv()
        rows = last_rows(SPOT_Z, SPOT_Z + BLK)
        last_sum[0] = dot(rows, eff[2, :BLK])
        last_sum[1] = dot(rows, mate_far[...])

    @pl.when(jnp.logical_not(has_from))
    def _():
        last_sum[...] = jnp.zeros_like(last_sum)

    acc[...] += dot(stack(cor_x, 0, nb, 0, HB), eff[1, :HB])
    middle = nb * BLK // 2
    stage3(late_x[0])
    last_sum[0] += dot(last_rows(0, middle), eff[0, :middle])
    last_sum[1] += dot(last_rows(0, middle), pair_e[:middle])
    stage3(late_x[1])
    for n, effects in enumerate((eff.at[0], pair_e)):
        value = last_sum[n] + dot(last_rows(middle, nb * BLK), effects[middle:])
        last_out[n] = value.astype(BF16)
        hops_last[n].start()

    for group in late_x:
        stage4(group)
    value = gram(late(0, nb * BLK), eff[1, HB:BLK])
    for u in range(nb):
        out_ref[at_block(mine(u)), :] = acc[block(u), :] + value[block(u)]
    remote(eff.at[1], eff.at[1], ex_send.at[0], ex_recv.at[0], partner, s).wait_send()

    @pl.when(has_to)
    def _():
        remote(eff.at[2], eff.at[2], ez_send.at[0], ez_recv.at[0], z_to, s).wait_send()

    finish(late_x)

    @pl.when(has_from)
    def _():
        finish([late_z, late_w])

    for t in range(1, nb):
        hops_x[t - 1].wait_recv()
        out_ref[at_block(other(t)), :] += hop_in[0, t].astype(F32)

    @pl.when(has_to)
    def _():
        for v in list(range(last - 1, -1, -1)) + [last]:
            hops_z[v].wait_recv()
            if v == last:
                hops_z[nb].wait_recv()
            out_ref[at_block(mine(v)), :] += hop_in[1, v].astype(F32)

    hops_x[nb - 1].wait_recv()
    first = pl.ds(pl.multiple_of(other(0) * BLK, BLK), HB)
    out_ref[first, :] += hop_in[0, 0, :HB].astype(F32)
    for n, c in enumerate(last_arrivals):
        c.wait_recv()
        rows = pl.ds(pl.multiple_of(other(0) * BLK + HB + n * (HB // 2), HB // 2), HB // 2)
        out_ref[rows, :] += last_in[n].astype(F32)
    for c in hops_x + hops_last:
        c.wait_send()

    @pl.when(has_from)
    def _():
        remote(hop_out.at[1], hop_in.at[1], h_send.at[1, 0], h_recv.at[1, 0], z_from, s).wait_send()


def body(n_genome, n_samp, dosage, effects, depth):
    nb = depth.shape[0]
    samples, variants = dosage.shape
    traits = effects.shape[1]
    half = samples // 2
    dma = pltpu.SemaphoreType.DMA
    pairs = nb * (nb + 1) // 2
    n_groups = 2 + sum(len(step) for steps in make_groups(nb)[:2] for step in steps)

    def pair_of(kind, lead, dtype):
        wide = pltpu.VMEM((nb,) + lead + (HB, variants), dtype)
        return [
            wide, wide, pltpu.VMEM((1,) + lead + (HB // 2, (nb + 3) * BLK), dtype), pltpu.VMEM((pairs,) + lead + (HB, BLK), kind),
        ]

    return pl.pallas_call(
        functools.partial(kernel, n_genome, n_samp, nb, half, 1.0 / (samples * n_samp)),
        out_shape=pltpu.VMEM((variants, traits), F32),
        in_specs=[
            pl.BlockSpec(memory_space=pl.ANY),
            pl.BlockSpec(memory_space=pl.ANY),
            pl.BlockSpec(memory_space=pltpu.SMEM),
        ],
        out_specs=pl.BlockSpec(memory_space=pltpu.VMEM),
        scratch_shapes=[
            pltpu.VMEM((8, BLK), F32),
            pltpu.VMEM((2, 8, BLK), F32),
            pltpu.VMEM((nb, samples, BLK), BF16),
            pltpu.VMEM((nb, half, BLK), BF16),
            pltpu.VMEM((nb, half, BLK), BF16),
            pltpu.VMEM((3, variants, traits), BF16),
            *pair_of(F32, (2,), F32),
            *pair_of(F32, (), F32),
            *pair_of(F32, (), BF16),
            *pair_of(F32, (), BF16),
            *pair_of(BF16, (2,), BF16),
            pltpu.VMEM((variants, traits), F32),
            pltpu.VMEM((variants, traits), F32),
            pltpu.VMEM((variants, traits), F32),
            pltpu.VMEM((2, nb, BLK, traits), BF16),
            pltpu.VMEM((2, nb, BLK, traits), BF16),
            pltpu.VMEM((variants, traits), BF16),
            pltpu.VMEM((BLK, traits), BF16),
            pltpu.VMEM((2, HB // 2, traits), F32),
            pltpu.VMEM((2, HB // 2, traits), BF16),
            pltpu.VMEM((2, HB // 2, traits), BF16),
            dma((1,)), dma((1,)),
            dma((1,)), dma((nb + len(PARTS),)),
            dma((1,)), dma((nb + len(PARTS),)),
            dma((1,)), dma((nb,)), dma((1,)), dma((nb,)), dma((2,)), dma((2,)),
            dma((n_groups,)), dma((n_groups,)), dma((n_groups,)), dma((n_groups,)), dma((n_groups,)), dma((n_groups,)),
            dma((2, nb + 1)), dma((2, nb + 1)), dma((2,)), dma((2,)), dma((2,)), dma((2,)),
        ],
        compiler_params=pltpu.CompilerParams(
            collective_id=0, has_side_effects=True, vmem_limit_bytes=60 * 1024 * 1024
        ),
        cost_estimate=pl.CostEstimate(
            flops=2 * 20 * BLK * BLK * samples, bytes_accessed=4 * samples * variants, transcendentals=0
        ),
    )(dosage, effects, depth)


def solution(mesh):
    return jax.shard_map(
        functools.partial(body, mesh.shape["genome"], mesh.shape["samp"]),
        mesh=mesh,
        in_specs=(P("samp", "genome"), P("genome", "samp"), P("genome")),
        out_specs=P("genome", "samp"),
        check_vma=False,
    )
```
